512 devices in a mesh: seq: 256 (over y, z_hi, x, core), head: 2 (over z_lo).
Axes of the slice: x: 4, y: 8, z: 8 (z_hi: 4, z_lo: 2; z = z_hi * 2 + z_lo), core: 2. Of those that a mesh axis runs over, the one named last changes fastest.
Arguments:
- queries: bfloat16 [32768, 8, 128], P('seq', 'head'), may hold values from -6 to 6
- keys: bfloat16 [32768, 128], P('seq'), may hold values from -6 to 6
- window_start: int32 [32768], P('seq'), may hold values from 0 to 32767, as said below
Outputs:
- gate_target: float32 [32768, 512], P('seq', 'head')
The draws below stay inside these ranges and needn't reach their ends.
Inputs may be any that keep to these rules, and one draw needn't show every extreme that they name: window_start[q] <= q for every position q.
All inputs are finite; a program needn't handle non-finite values.
Results may differ from the reference program's by a relative error of at most 0.0003.
Values may be sent and summed in bfloat16 or wider, within the bound.
No kernel may reach another device: no remote copies, remote signals or barrier semaphores. Data moves between devices by JAX's collectives and lax.ppermute only.
A program may use at most 64 MiB of HBM per device.

```python
import math
import jax
import jax.numpy as jnp
from jax import lax

D = 128
HEADS = 8
BLOCK = 64
TOKENS = 32768
NBLK = 512


def draw_queries(key, part):
    key = jax.random.fold_in(key, 1)
    base = jax.random.truncated_normal(key, -6.0, 6.0, (TOKENS, HEADS, D), jnp.float32)
    return base.astype(jnp.bfloat16)


def draw_keys(key, part):
    key = jax.random.fold_in(key, 2)
    base = jax.random.truncated_normal(key, -6.0, 6.0, (TOKENS, D), jnp.float32)
    return base.astype(jnp.bfloat16)


def draw_window_start(key, part):
    key = jax.random.fold_in(key, 3)
    places = jnp.arange(TOKENS, dtype=jnp.int32)
    starts = jax.random.randint(key, (TOKENS,), jnp.zeros((TOKENS,), jnp.int32), places + 1).astype(jnp.int32)
    return starts.at[TOKENS - 1].set(TOKENS - 1).astype(jnp.int32)


def setup_inputs(seed: int = 0) -> dict:
    key_list = jax.random.split(jax.random.key(seed), 4)
    queries = draw_queries(jax.random.fold_in(key_list[3], 71), 0)
    keys = draw_keys(jax.random.fold_in(key_list[3], 71), 0)
    window_start = draw_window_start(jax.random.fold_in(key_list[3], 71), 0)
    return dict(queries=queries, keys=keys, window_start=window_start)


def reference(queries, keys, window_start):
    scale = 1.0 / math.sqrt(D)
    group = math.gcd(TOKENS, 1024)
    sub = math.gcd(group, 256)
    results = []
    for index in range(TOKENS // group):
        end = (index + 1) * group
        key_rows = keys[:end].astype(jnp.float32)
        query_rows = queries[index * group:end].astype(jnp.float32).reshape(group // sub, sub, HEADS, D)
        starts = window_start[index * group:end].reshape(group // sub, sub)
        places = (index * group + jnp.arange(group, dtype=jnp.int32)).reshape(group // sub, sub)

        def one_block(args):
            query_block, start_block, place_block = args
            scores = jnp.einsum('qhd,kd->hqk', query_block, key_rows, precision=lax.Precision.HIGHEST) * scale
            key_place = jnp.arange(end, dtype=jnp.int32)
            allowed = (key_place[None, :] <= place_block[:, None]) & (key_place[None, :] >= start_block[:, None])
            masked = jnp.where(allowed[None], scores, -1e+30)
            top = lax.optimization_barrier(jnp.max(masked, axis=-1, keepdims=True))
            weights = jnp.where(allowed[None], jnp.exp(scores - top), 0.0)
            probs = weights / lax.optimization_barrier(jnp.sum(weights, axis=-1, keepdims=True))
            blocks = lax.optimization_barrier(jnp.sum(probs.reshape(HEADS, sub, end // BLOCK, BLOCK), axis=-1))
            blocks = lax.optimization_barrier(jnp.sum(blocks, axis=0)) / HEADS
            visible = (place_block // BLOCK - start_block // BLOCK + 1).astype(jnp.float32)
            target = blocks * visible[:, None]
            return jnp.pad(target, ((0, 0), (0, NBLK - end // BLOCK)))
        results.append(lax.map(one_block, (query_rows, starts, places)).reshape(group, NBLK))
    return jnp.concatenate(results, axis=0)
```

```python
import functools
import math

import jax
import jax.numpy as jnp
import numpy as np
from jax import lax
from jax.experimental import pallas as pl
from jax.experimental.pallas import tpu as pltpu
from jax.sharding import Mesh, PartitionSpec as P

BLOCK = 64
CHUNK = 16
LOW = -1e30
SAFE = 60.0
LOG2E = math.log2(math.e)


def shard_of(index, low, core):
    return index // 16 * 64 + low * 32 + index % 16 * 2 + core


def prepare_kernel(*refs, scale, rows):
    *q_refs, lines_ref, starts_ref, most_ref = refs
    mine = lax.axis_index(GROUP)
    depth = lines_ref.shape[0] // 2
    half = lines_ref.shape[1] // len(q_refs)
    most = jnp.float32(0.0)
    for slot, q_ref in enumerate(q_refs):
        source = mine ^ slot
        raw = q_ref[0:depth, :].astype(jnp.float32)
        most = jnp.maximum(most, jnp.max(jnp.sum(raw * raw, axis=0, keepdims=True)))
        scaled = raw * (scale * LOG2E)
        high = scaled.astype(jnp.bfloat16)
        low = (scaled - high.astype(jnp.float32)).astype(jnp.bfloat16)
        at = pl.ds(pl.multiple_of(source * half, half), half)
        lines_ref[0:depth, at] = high
        lines_ref[depth : 2 * depth, at] = low
        digits = q_ref[depth : depth + 16, 0:rows].astype(jnp.float32)
        starts_ref[pl.ds(source, 1), :] = (digits[0:1, :] * 256.0 + digits[1:2, :]).astype(jnp.int32)
    most_ref[...] = jnp.full_like(most_ref, most)


def score_kernel(most_ref, starts_ref, lines_ref, keys_ref, sums_ref, stat_ref, *refs, members, heads, rows, scale, swap):
    mask_ref, tile_ref, part_ref, top_ref = refs
    group = lax.axis_index(PLACE)
    mine = lax.axis_index(GROUP)
    core = lax.axis_index("core")
    side = core ^ swap
    span = CHUNK * BLOCK
    width = heads * rows
    pair = 2 * rows

    largest = jnp.max(jnp.abs(keys_ref[...]), axis=1).astype(jnp.float32)
    longest = jnp.max(jnp.sum(largest * largest, axis=-1))
    safe = jnp.max(most_ref[...]) * longest * (scale * scale) <= SAFE * SAFE
    sums_ref[...] = jnp.zeros_like(sums_ref)

    starts = [starts_ref[2 * member : 2 * member + 1, :] for member in range(members)]
    first_start = jnp.min(functools.reduce(jnp.minimum, starts))
    last_chunk = group // CHUNK
    first_chunk = jnp.minimum(first_start // (rows * 64), last_chunk)

    def chunk_keys(chunk):
        blocks = [keys_ref[column, chunk * 4 + step] for step in range(4) for column in range(4)]
        keys = jnp.concatenate(blocks, axis=0)
        return jnp.concatenate([keys, keys], axis=1)

    line = lax.broadcasted_iota(jnp.int32, (BLOCK, rows), 0)
    places = [
        shard_of(group, member, core) * rows + lax.broadcasted_iota(jnp.int32, (1, rows), 1) for member in range(members)
    ]

    def fill_mask(chunk, inside, outside):
        for block in range(CHUNK):
            base = (shard_of(chunk * CHUNK + block, mine // 2, side) * 2 + mine % 2) * BLOCK
            for member in range(members):
                allowed = (line >= starts[member] - base) & (line <= places[member] - base)
                mask_ref[member, block * BLOCK : (block + 1) * BLOCK, :] = jnp.where(allowed, inside, outside)

    def scores(keys, at):
        return jnp.dot(keys, lines_ref[:, pl.ds(at, pair)], preferred_element_type=jnp.float32)

    def lines_of(chunk):
        return pl.ds(pl.multiple_of(chunk * CHUNK, CHUNK), CHUNK)

    @pl.when(safe)
    def _():
        def one_chunk(chunk, carry):
            keys = chunk_keys(chunk)
            fill_mask(chunk, 1.0, 0.0)
            tile_ref[0] = scores(keys, 0)
            for tile in range(members * width // pair):
                at = tile * pair
                if at + pair < members * width:
                    tile_ref[(tile + 1) % 2] = scores(keys, at + pair)
                for block in range(CHUNK):
                    lines = slice(block * BLOCK, (block + 1) * BLOCK)
                    mask = mask_ref[at // width, lines, :]
                    for column in range(2):
                        x = tile_ref[tile % 2, lines, column * rows : (column + 1) * rows]
                        weights = jnp.exp2(x) * mask
                        part_ref[2 * tile + column, block * 8 : block * 8 + 8, :] = jnp.sum(
                            weights.reshape(BLOCK // 8, 8, rows), axis=0
                        )
                for column in range(2):
                    total = part_ref[2 * tile + column, pl.ds(0, CHUNK, stride=8), :]
                    for line in range(1, 8):
                        total = total + part_ref[2 * tile + column, pl.ds(line, CHUNK, stride=8), :]
                    sums_ref[lines_of(chunk), at + column * rows : at + (column + 1) * rows] = total
            return carry

        lax.fori_loop(first_chunk, last_chunk + 1, one_chunk, 0)

    def each_tile(visit):
        def one_chunk(chunk, carry):
            fill_mask(chunk, 0.0, LOW)

            def one_tile(tile, carry):
                at = pl.multiple_of(tile * pair, pair)
                mask = mask_ref[at // width]
                visit(chunk, pl.ds(at, pair), scores(chunk_keys(chunk), at) + jnp.concatenate([mask, mask], axis=1))
                return carry

            return lax.fori_loop(0, members * width // pair, one_tile, carry)

        lax.fori_loop(first_chunk, last_chunk + 1, one_chunk, 0)

    @pl.when(jnp.logical_not(safe))
    def _():
        def raise_top(chunk, at, x):
            top_ref[:, at] = jnp.maximum(top_ref[:, at], jnp.max(x, axis=0, keepdims=True))

        def add(chunk, at, x):
            weights = jnp.where(x > 0.5 * LOW, jnp.exp2(jnp.minimum(x - top_ref[:, at], 0.0)), 0.0)
            sums_ref[lines_of(chunk), at] = jnp.sum(weights.reshape(CHUNK, BLOCK, pair), axis=1)

        top_ref[...] = jnp.full_like(top_ref, LOW)
        each_tile(raise_top)
        each_tile(add)

    total = jnp.sum(sums_ref[...], axis=0, keepdims=True)
    top = jnp.where(safe, jnp.zeros_like(total), top_ref[...])
    stat_ref[0:1, :] = jnp.where(total > 0.0, top, LOW)
    stat_ref[1:2, :] = total


def mass_kernel(own_ref, other_ref, stat_ref, mass_ref, *, members, heads, rows):
    mine = lax.axis_index(GROUP)
    tops = [stat_ref[:, 0, :], stat_ref[:, 2, :]]
    top = jnp.max(jnp.maximum(*tops), axis=0, keepdims=True)
    total = stat_ref[:, 1, :] * jnp.exp2(tops[0] - top) + stat_ref[:, 3, :] * jnp.exp2(tops[1] - top)
    total = jnp.sum(total, axis=0, keepdims=True)
    for side, sums_ref in enumerate((own_ref, other_ref)):
        share = jnp.exp2(stat_ref[mine, 2 * side : 2 * side + 1, :] - top) / total
        for member in range(members):
            mass = None
            for head in range(heads):
                at = (member * heads + head) * rows
                term = sums_ref[:, at : at + rows] * share[:, at : at + rows]
                mass = term if mass is None else mass + term
            for run in range(mass_ref.shape[1]):
                mass_ref[member, run, side] = mass[run * 16 : run * 16 + 16, :]


def target_kernel(mass_ref, ws_ref, out_ref, lines_ref, *, devices, rows, heads):
    core = lax.axis_index("core")
    first = shard_of(lax.axis_index(PLACE), lax.axis_index("yl"), core) * rows
    place = first + lax.broadcasted_iota(jnp.int32, (1, rows), 1)
    visible = (place // BLOCK - ws_ref[...] // BLOCK + 1).astype(jnp.float32) * (1.0 / heads)
    for source in range(devices):
        for run in range(mass_ref.shape[1]):
            for side in range(2):
                begin = 2 * shard_of(run * 16, source // 2, core ^ side) + source % 2
                lines_ref[pl.ds(begin, 16, stride=4), :] = mass_ref[source, run, side] * visible
    out_ref[...] = lines_ref[...].T


GROUP = ("yl", "head")
PLACE = ("yh", "zh", "x")


def spread(x, axes):
    copies = jnp.broadcast_to(x[None], (lax.axis_size(axes), *x.shape))
    return lax.all_to_all(copies, axes, 0, 0, tiled=True)


def body(queries, keys, window_start):
    blocks = lax.axis_size(PLACE)
    devices = lax.axis_size(GROUP)
    members = devices // 2
    rows, heads_here, width = queries.shape
    heads = 2 * heads_here
    scale = 1.0 / math.sqrt(width)

    lines = jnp.transpose(queries, (2, 1, 0)).reshape(width, heads_here * rows)
    digits = jnp.stack([window_start // 256, window_start % 256]).astype(jnp.bfloat16)
    digits = jnp.pad(digits, ((0, 14), (0, (heads_here - 1) * rows)))
    lines = jnp.concatenate([lines, digits], axis=0)
    def trade(x, step):
        return lax.ppermute(x, GROUP, [(i, i ^ step) for i in range(devices)])

    own = lax.dynamic_slice_in_dim(keys, lax.axis_index("head") * BLOCK, BLOCK, 0)
    column, lines, across, along = lax.optimization_barrier(
        (spread(own, ("yh", "zh")), lines, trade(lines, 3), trade(lines, 2))
    )
    own_keys = spread(column, "x")
    all_queries = [lines, trade(lines, 1), along, across]

    total_rows = members * heads * rows
    vmem = pl.BlockSpec(memory_space=pltpu.VMEM)
    params = pltpu.CompilerParams(vmem_limit_bytes=32 * 1024 * 1024)

    query_lines, starts, most = pl.pallas_call(
        functools.partial(prepare_kernel, scale=scale, rows=rows),
        out_shape=(
            jax.ShapeDtypeStruct((2 * width, total_rows), jnp.bfloat16),
            jax.ShapeDtypeStruct((devices, rows), jnp.int32),
            jax.ShapeDtypeStruct((8, rows), jnp.float32),
        ),
        in_specs=[vmem] * devices,
        out_specs=(vmem, vmem, vmem),
        compiler_params=params,
        cost_estimate=pl.CostEstimate(flops=10 * width * total_rows, bytes_accessed=2 * 1024 * 1024, transcendentals=0),
        name="prepare",
    )(*all_queries)

    own_keys, query_lines = lax.optimization_barrier((own_keys, query_lines))
    other_keys = lax.ppermute(own_keys, "core", [(0, 1), (1, 0)])

    def score(half_keys, swap):
        return pl.pallas_call(
            functools.partial(score_kernel, members=members, heads=heads, rows=rows, scale=scale, swap=swap),
            out_shape=(
                jax.ShapeDtypeStruct((blocks, total_rows), jnp.float32),
                jax.ShapeDtypeStruct((2, total_rows), jnp.float32),
            ),
            in_specs=[vmem] * 4,
            out_specs=(vmem, vmem),
            scratch_shapes=[
                pltpu.VMEM((members, CHUNK * BLOCK, rows), jnp.float32),
                pltpu.VMEM((2, CHUNK * BLOCK, 2 * rows), jnp.float32),
                pltpu.VMEM((total_rows // rows, CHUNK * 8, rows), jnp.float32),
                pltpu.VMEM((1, total_rows), jnp.float32),
            ],
            compiler_params=params,
            cost_estimate=pl.CostEstimate(
                flops=2 * blocks * BLOCK * width * total_rows,
                bytes_accessed=8 * 1024 * 1024,
                transcendentals=blocks * BLOCK * total_rows,
            ),
            name="score",
        )(most, starts, query_lines, half_keys)

    own_sums, own_stat = score(own_keys, 0)
    other_sums, other_stat = score(other_keys, 1)
    stats = spread(jnp.concatenate([own_stat, other_stat], axis=0), GROUP)
    mass = pl.pallas_call(
        functools.partial(mass_kernel, members=members, heads=heads, rows=rows),
        out_shape=jax.ShapeDtypeStruct((members, blocks // 16, 2, 16, rows), jnp.float32),
        in_specs=[vmem] * 3,
        out_specs=vmem,
        compiler_params=params,
        name="mass",
    )(own_sums, other_sums, stats)
    mass = mass.reshape(devices, blocks // 32, 2, 16, rows)
    mass = lax.all_to_all(mass, GROUP, 0, 0, tiled=True)
    return pl.pallas_call(
        functools.partial(target_kernel, devices=devices, rows=rows, heads=heads),
        out_shape=jax.ShapeDtypeStruct((rows, blocks * devices), jnp.float32),
        in_specs=[vmem] * 2,
        out_specs=vmem,
        scratch_shapes=[pltpu.VMEM((blocks * devices, rows), jnp.float32)],
        compiler_params=params,
        name="target",
    )(mass, window_start.reshape(1, rows))


def solution(mesh):
    grid = Mesh(mesh.devices.reshape(-1, 2, 4, 4, 2, 2), ("yh", "yl", "zh", "x", "core", "head"))
    seq = ("yh", "yl", "zh", "x", "core")
    placed = (P(seq, "head", None), P(seq, None), P(seq))
    return jax.shard_map(body, mesh=grid, in_specs=placed, out_specs=P(seq, "head"), check_vma=False)
```

```python
import functools
import math

import jax
import jax.numpy as jnp
import numpy as np
from jax import lax
from jax.experimental import pallas as pl
from jax.experimental.pallas import tpu as pltpu
from jax.sharding import Mesh, PartitionSpec as P

BLOCK = 64
CHUNK = 16
LOW = -1e30
SAFE = 60.0
LOG2E = math.log2(math.e)


def shard_of(index, low, core):
    return index // 16 * 64 + low * 32 + index % 16 * 2 + core


def prepare_kernel(*refs, scale, rows):
    *q_refs, lines_ref, starts_ref, most_ref = refs
    mine = lax.axis_index(GROUP)
    depth = lines_ref.shape[0] // 2
    half = lines_ref.shape[1] // len(q_refs)
    most = jnp.float32(0.0)
    for slot, q_ref in enumerate(q_refs):
        source = mine ^ slot
        raw = q_ref[0:depth, :].astype(jnp.float32)
        most = jnp.maximum(most, jnp.max(jnp.sum(raw * raw, axis=0, keepdims=True)))
        scaled = raw * (scale * LOG2E)
        high = scaled.astype(jnp.bfloat16)
        low = (scaled - high.astype(jnp.float32)).astype(jnp.bfloat16)
        at = pl.ds(pl.multiple_of(source * half, half), half)
        lines_ref[0:depth, at] = high
        lines_ref[depth : 2 * depth, at] = low
        digits = q_ref[depth : depth + 16, 0:rows].astype(jnp.float32)
        starts_ref[pl.ds(source, 1), :] = (digits[0:1, :] * 256.0 + digits[1:2, :]).astype(jnp.int32)
    most_ref[...] = jnp.full_like(most_ref, most)


def score_kernel(most_ref, starts_ref, lines_ref, keys_ref, sums_ref, stat_ref, *refs, members, heads, rows, scale, swap):
    mask_ref, tile_ref, part_ref, top_ref = refs
    group = lax.axis_index(PLACE)
    mine = lax.axis_index(GROUP)
    core = lax.axis_index("core")
    side = core ^ swap
    span = CHUNK * BLOCK
    width = heads * rows
    pair = 2 * rows

    largest = jnp.max(jnp.abs(keys_ref[...]), axis=1).astype(jnp.float32)
    longest = jnp.max(jnp.sum(largest * largest, axis=-1))
    safe = jnp.max(most_ref[...]) * longest * (scale * scale) <= SAFE * SAFE
    sums_ref[...] = jnp.zeros_like(sums_ref)

    starts = [starts_ref[2 * member : 2 * member + 1, :] for member in range(members)]
    first_start = jnp.min(functools.reduce(jnp.minimum, starts))
    last_chunk = group // CHUNK
    first_chunk = jnp.minimum(first_start // (rows * 64), last_chunk)

    def chunk_keys(chunk):
        blocks = [keys_ref[column, chunk * 4 + step] for step in range(4) for column in range(4)]
        keys = jnp.concatenate(blocks, axis=0)
        return jnp.concatenate([keys, keys], axis=1)

    line = lax.broadcasted_iota(jnp.int32, (BLOCK, rows), 0)
    places = [
        shard_of(group, member, core) * rows + lax.broadcasted_iota(jnp.int32, (1, rows), 1) for member in range(members)
    ]

    def fill_mask(chunk, inside, outside):
        for block in range(CHUNK):
            base = (shard_of(chunk * CHUNK + block, mine // 2, side) * 2 + mine % 2) * BLOCK
            for member in range(members):
                allowed = (line >= starts[member] - base) & (line <= places[member] - base)
                mask_ref[member, block * BLOCK : (block + 1) * BLOCK, :] = jnp.where(allowed, inside, outside)

    def scores(keys, at):
        return jnp.dot(keys, lines_ref[:, pl.ds(at, pair)], preferred_element_type=jnp.float32)

    def lines_of(chunk):
        return pl.ds(pl.multiple_of(chunk * CHUNK, CHUNK), CHUNK)

    @pl.when(safe)
    def _():
        def one_chunk(chunk, carry):
            keys = chunk_keys(chunk)
            fill_mask(chunk, 1.0, 0.0)
            tile_ref[0] = scores(keys, 0)
            for tile in range(members * width // pair):
                at = tile * pair
                if at + pair < members * width:
                    tile_ref[(tile + 1) % 2] = scores(keys, at + pair)
                for block in range(CHUNK):
                    lines = slice(block * BLOCK, (block + 1) * BLOCK)
                    mask = mask_ref[at // width, lines, :]
                    for column in range(2):
                        x = tile_ref[tile % 2, lines, column * rows : (column + 1) * rows]
                        weights = jnp.exp2(x) * mask
                        part_ref[2 * tile + column, block * 8 : block * 8 + 8, :] = jnp.sum(
                            weights.reshape(BLOCK // 8, 8, rows), axis=0
                        )
                for column in range(2):
                    total = part_ref[2 * tile + column, pl.ds(0, CHUNK, stride=8), :]
                    for line in range(1, 8):
                        total = total + part_ref[2 * tile + column, pl.ds(line, CHUNK, stride=8), :]
                    sums_ref[lines_of(chunk), at + column * rows : at + (column + 1) * rows] = total
            return carry

        lax.fori_loop(first_chunk, last_chunk + 1, one_chunk, 0)

    def each_tile(visit):
        def one_chunk(chunk, carry):
            fill_mask(chunk, 0.0, LOW)

            def one_tile(tile, carry):
                at = pl.multiple_of(tile * pair, pair)
                mask = mask_ref[at // width]
                visit(chunk, pl.ds(at, pair), scores(chunk_keys(chunk), at) + jnp.concatenate([mask, mask], axis=1))
                return carry

            return lax.fori_loop(0, members * width // pair, one_tile, carry)

        lax.fori_loop(first_chunk, last_chunk + 1, one_chunk, 0)

    @pl.when(jnp.logical_not(safe))
    def _():
        def raise_top(chunk, at, x):
            top_ref[:, at] = jnp.maximum(top_ref[:, at], jnp.max(x, axis=0, keepdims=True))

        def add(chunk, at, x):
            weights = jnp.where(x > 0.5 * LOW, jnp.exp2(jnp.minimum(x - top_ref[:, at], 0.0)), 0.0)
            sums_ref[lines_of(chunk), at] = jnp.sum(weights.reshape(CHUNK, BLOCK, pair), axis=1)

        top_ref[...] = jnp.full_like(top_ref, LOW)
        each_tile(raise_top)
        each_tile(add)

    total = jnp.sum(sums_ref[...], axis=0, keepdims=True)
    top = jnp.where(safe, jnp.zeros_like(total), top_ref[...])
    stat_ref[0:1, :] = jnp.where(total > 0.0, top, LOW)
    stat_ref[1:2, :] = total


def mass_kernel(own_ref, other_ref, stat_ref, mass_ref, *, members, heads, rows):
    mine = lax.axis_index(GROUP)
    tops = [stat_ref[:, 0, :], stat_ref[:, 2, :]]
    top = jnp.max(jnp.maximum(*tops), axis=0, keepdims=True)
    total = stat_ref[:, 1, :] * jnp.exp2(tops[0] - top) + stat_ref[:, 3, :] * jnp.exp2(tops[1] - top)
    total = jnp.sum(total, axis=0, keepdims=True)
    for side, sums_ref in enumerate((own_ref, other_ref)):
        share = jnp.exp2(stat_ref[mine, 2 * side : 2 * side + 1, :] - top) / total
        for member in range(members):
            mass = None
            for head in range(heads):
                at = (member * heads + head) * rows
                term = sums_ref[:, at : at + rows] * share[:, at : at + rows]
                mass = term if mass is None else mass + term
            for run in range(mass_ref.shape[1]):
                mass_ref[member, run, side] = mass[run * 16 : run * 16 + 16, :]


def target_kernel(mass_ref, ws_ref, out_ref, lines_ref, *, devices, rows, heads):
    core = lax.axis_index("core")
    first = shard_of(lax.axis_index(PLACE), lax.axis_index("yl"), core) * rows
    place = first + lax.broadcasted_iota(jnp.int32, (1, rows), 1)
    visible = (place // BLOCK - ws_ref[...] // BLOCK + 1).astype(jnp.float32) * (1.0 / heads)
    for source in range(devices):
        for run in range(mass_ref.shape[1]):
            for side in range(2):
                begin = 2 * shard_of(run * 16, source // 2, core ^ side) + source % 2
                lines_ref[pl.ds(begin, 16, stride=4), :] = mass_ref[source, run, side] * visible
    out_ref[...] = lines_ref[...].T


GROUP = ("yl", "head")
PLACE = ("yh", "zh", "x")


def spread(x, axes):
    copies = jnp.broadcast_to(x[None], (lax.axis_size(axes), *x.shape))
    return lax.all_to_all(copies, axes, 0, 0, tiled=True)


def body(queries, keys, window_start):
    blocks = lax.axis_size(PLACE)
    devices = lax.axis_size(GROUP)
    members = devices // 2
    rows, heads_here, width = queries.shape
    heads = 2 * heads_here
    scale = 1.0 / math.sqrt(width)

    lines = jnp.transpose(queries, (2, 1, 0)).reshape(width, heads_here * rows)
    digits = jnp.stack([window_start // 256, window_start % 256]).astype(jnp.bfloat16)
    digits = jnp.pad(digits, ((0, 14), (0, (heads_here - 1) * rows)))
    lines = jnp.concatenate([lines, digits], axis=0)

    def trade(x, step):
        return lax.ppermute(x, GROUP, [(i, i ^ step) for i in range(devices)])

    own = lax.dynamic_slice_in_dim(keys, lax.axis_index("head") * BLOCK, BLOCK, 0)
    column, lines, near = lax.optimization_barrier((spread(own, ("yh", "zh")), lines, trade(lines, 1)))
    own_keys = spread(column, "x")
    across, along = trade(lines, 3), trade(lines, 2)
    all_queries = [lines, near, along, across]

    total_rows = members * heads * rows
    vmem = pl.BlockSpec(memory_space=pltpu.VMEM)
    params = pltpu.CompilerParams(vmem_limit_bytes=32 * 1024 * 1024)

    query_lines, starts, most = pl.pallas_call(
        functools.partial(prepare_kernel, scale=scale, rows=rows),
        out_shape=(
            jax.ShapeDtypeStruct((2 * width, total_rows), jnp.bfloat16),
            jax.ShapeDtypeStruct((devices, rows), jnp.int32),
            jax.ShapeDtypeStruct((8, rows), jnp.float32),
        ),
        in_specs=[vmem] * devices,
        out_specs=(vmem, vmem, vmem),
        compiler_params=params,
        cost_estimate=pl.CostEstimate(flops=10 * width * total_rows, bytes_accessed=2 * 1024 * 1024, transcendentals=0),
        name="prepare",
    )(*all_queries)

    own_keys, query_lines = lax.optimization_barrier((own_keys, query_lines))
    other_keys = lax.ppermute(own_keys, "core", [(0, 1), (1, 0)])

    def score(half_keys, swap):
        return pl.pallas_call(
            functools.partial(score_kernel, members=members, heads=heads, rows=rows, scale=scale, swap=swap),
            out_shape=(
                jax.ShapeDtypeStruct((blocks, total_rows), jnp.float32),
                jax.ShapeDtypeStruct((2, total_rows), jnp.float32),
            ),
            in_specs=[vmem] * 4,
            out_specs=(vmem, vmem),
            scratch_shapes=[
                pltpu.VMEM((members, CHUNK * BLOCK, rows), jnp.float32),
                pltpu.VMEM((2, CHUNK * BLOCK, 2 * rows), jnp.float32),
                pltpu.VMEM((total_rows // rows, CHUNK * 8, rows), jnp.float32),
                pltpu.VMEM((1, total_rows), jnp.float32),
            ],
            compiler_params=params,
            cost_estimate=pl.CostEstimate(
                flops=2 * blocks * BLOCK * width * total_rows,
                bytes_accessed=8 * 1024 * 1024,
                transcendentals=blocks * BLOCK * total_rows,
            ),
            name="score",
        )(most, starts, query_lines, half_keys)

    own_sums, own_stat = score(own_keys, 0)
    other_sums, other_stat = score(other_keys, 1)
    stats = spread(jnp.concatenate([own_stat, other_stat], axis=0), GROUP)
    mass = pl.pallas_call(
        functools.partial(mass_kernel, members=members, heads=heads, rows=rows),
        out_shape=jax.ShapeDtypeStruct((members, blocks // 16, 2, 16, rows), jnp.float32),
        in_specs=[vmem] * 3,
        out_specs=vmem,
        compiler_params=params,
        name="mass",
    )(own_sums, other_sums, stats)
    mass = mass.reshape(devices, blocks // 32, 2, 16, rows)
    mass = lax.all_to_all(mass, GROUP, 0, 0, tiled=True)
    return pl.pallas_call(
        functools.partial(target_kernel, devices=devices, rows=rows, heads=heads),
        out_shape=jax.ShapeDtypeStruct((rows, blocks * devices), jnp.float32),
        in_specs=[vmem] * 2,
        out_specs=vmem,
        scratch_shapes=[pltpu.VMEM((blocks * devices, rows), jnp.float32)],
        compiler_params=params,
        name="target",
    )(mass, window_start.reshape(1, rows))


def solution(mesh):
    grid = Mesh(mesh.devices.reshape(-1, 2, 4, 4, 2, 2), ("yh", "yl", "zh", "x", "core", "head"))
    seq = ("yh", "yl", "zh", "x", "core")
    placed = (P(seq, "head", None), P(seq, None), P(seq))
    return jax.shard_map(body, mesh=grid, in_specs=placed, out_specs=P(seq, "head"), check_vma=False)
```

```python
import functools
import math

import jax
import jax.numpy as jnp
import numpy as np
from jax import lax
from jax.experimental import pallas as pl
from jax.experimental.pallas import tpu as pltpu
from jax.sharding import Mesh, PartitionSpec as P

BLOCK = 64
CHUNK = 16
LOW = -1e30
SAFE = 60.0
LOG2E = math.log2(math.e)


def shard_of(index, low, core):
    return index // 16 * 64 + low * 32 + index % 16 * 2 + core


def prepare_kernel(*refs, scale, rows):
    *q_refs, lines_ref, starts_ref, most_ref = refs
    mine = lax.axis_index(GROUP)
    depth = lines_ref.shape[0] // 2
    half = lines_ref.shape[1] // len(q_refs)
    most = jnp.float32(0.0)
    for slot, q_ref in enumerate(q_refs):
        source = mine ^ slot
        raw = q_ref[0:depth, :].astype(jnp.float32)
        most = jnp.maximum(most, jnp.max(jnp.sum(raw * raw, axis=0, keepdims=True)))
        scaled = raw * (scale * LOG2E)
        high = scaled.astype(jnp.bfloat16)
        low = (scaled - high.astype(jnp.float32)).astype(jnp.bfloat16)
        at = pl.ds(pl.multiple_of(source * half, half), half)
        lines_ref[0:depth, at] = high
        lines_ref[depth : 2 * depth, at] = low
        digits = q_ref[depth : depth + 16, 0:rows].astype(jnp.float32)
        starts_ref[pl.ds(source, 1), :] = (digits[0:1, :] * 256.0 + digits[1:2, :]).astype(jnp.int32)
    most_ref[...] = jnp.full_like(most_ref, most)


def score_kernel(most_ref, starts_ref, lines_ref, keys_ref, sums_ref, stat_ref, *refs, members, heads, rows, scale, swap):
    mask_ref, tile_ref, part_ref, top_ref = refs
    group = lax.axis_index(PLACE)
    mine = lax.axis_index(GROUP)
    core = lax.axis_index("core")
    side = core ^ swap
    span = CHUNK * BLOCK
    width = heads * rows
    pair = 2 * rows

    largest = jnp.max(jnp.abs(keys_ref[...]), axis=1).astype(jnp.float32)
    longest = jnp.max(jnp.sum(largest * largest, axis=-1))
    safe = jnp.max(most_ref[...]) * longest * (scale * scale) <= SAFE * SAFE
    sums_ref[...] = jnp.zeros_like(sums_ref)

    starts = [starts_ref[2 * member : 2 * member + 1, :] for member in range(members)]
    first_start = jnp.min(functools.reduce(jnp.minimum, starts))
    last_chunk = group // CHUNK
    first_chunk = jnp.minimum(first_start // (rows * 64), last_chunk)

    def chunk_keys(chunk):
        blocks = [keys_ref[column, chunk * 4 + step] for step in range(4) for column in range(4)]
        keys = jnp.concatenate(blocks, axis=0)
        return jnp.concatenate([keys, keys], axis=1)

    line = lax.broadcasted_iota(jnp.int32, (BLOCK, rows), 0)
    places = [
        shard_of(group, member, core) * rows + lax.broadcasted_iota(jnp.int32, (1, rows), 1) for member in range(members)
    ]

    def fill_mask(chunk, inside, outside):
        for block in range(CHUNK):
            base = (shard_of(chunk * CHUNK + block, mine // 2, side) * 2 + mine % 2) * BLOCK
            for member in range(members):
                allowed = (line >= starts[member] - base) & (line <= places[member] - base)
                mask_ref[member, block * BLOCK : (block + 1) * BLOCK, :] = jnp.where(allowed, inside, outside)

    def scores(keys, at):
        return jnp.dot(keys, lines_ref[:, pl.ds(at, pair)], preferred_element_type=jnp.float32)

    def lines_of(chunk):
        return pl.ds(pl.multiple_of(chunk * CHUNK, CHUNK), CHUNK)

    @pl.when(safe)
    def _():
        def one_chunk(chunk, carry):
            keys = chunk_keys(chunk)
            fill_mask(chunk, 1.0, 0.0)
            tile_ref[0] = scores(keys, 0)
            for tile in range(members * width // pair):
                at = tile * pair
                if at + pair < members * width:
                    tile_ref[(tile + 1) % 2] = scores(keys, at + pair)
                for block in range(CHUNK):
                    lines = slice(block * BLOCK, (block + 1) * BLOCK)
                    mask = mask_ref[at // width, lines, :]
                    for column in range(2):
                        x = tile_ref[tile % 2, lines, column * rows : (column + 1) * rows]
                        weights = jnp.exp2(x) * mask
                        part_ref[2 * tile + column, block * 8 : block * 8 + 8, :] = jnp.sum(
                            weights.reshape(BLOCK // 8, 8, rows), axis=0
                        )
                for column in range(2):
                    total = part_ref[2 * tile + column, pl.ds(0, CHUNK, stride=8), :]
                    for line in range(1, 8):
                        total = total + part_ref[2 * tile + column, pl.ds(line, CHUNK, stride=8), :]
                    sums_ref[lines_of(chunk), at + column * rows : at + (column + 1) * rows] = total
            return carry

        lax.fori_loop(first_chunk, last_chunk + 1, one_chunk, 0)

    def each_tile(visit):
        def one_chunk(chunk, carry):
            fill_mask(chunk, 0.0, LOW)

            def one_tile(tile, carry):
                at = pl.multiple_of(tile * pair, pair)
                mask = mask_ref[at // width]
                visit(chunk, pl.ds(at, pair), scores(chunk_keys(chunk), at) + jnp.concatenate([mask, mask], axis=1))
                return carry

            return lax.fori_loop(0, members * width // pair, one_tile, carry)

        lax.fori_loop(first_chunk, last_chunk + 1, one_chunk, 0)

    @pl.when(jnp.logical_not(safe))
    def _():
        def raise_top(chunk, at, x):
            top_ref[:, at] = jnp.maximum(top_ref[:, at], jnp.max(x, axis=0, keepdims=True))

        def add(chunk, at, x):
            weights = jnp.where(x > 0.5 * LOW, jnp.exp2(jnp.minimum(x - top_ref[:, at], 0.0)), 0.0)
            sums_ref[lines_of(chunk), at] = jnp.sum(weights.reshape(CHUNK, BLOCK, pair), axis=1)

        top_ref[...] = jnp.full_like(top_ref, LOW)
        each_tile(raise_top)
        each_tile(add)

    total = jnp.sum(sums_ref[...], axis=0, keepdims=True)
    top = jnp.where(safe, jnp.zeros_like(total), top_ref[...])
    stat_ref[0:1, :] = jnp.where(total > 0.0, top, LOW)
    stat_ref[1:2, :] = total


def mass_kernel(own_ref, other_ref, stat_ref, mass_ref, *, members, heads, rows):
    mine = lax.axis_index(GROUP)
    tops = [stat_ref[:, 0, :], stat_ref[:, 2, :]]
    top = jnp.max(jnp.maximum(*tops), axis=0, keepdims=True)
    total = stat_ref[:, 1, :] * jnp.exp2(tops[0] - top) + stat_ref[:, 3, :] * jnp.exp2(tops[1] - top)
    total = jnp.sum(total, axis=0, keepdims=True)
    for side, sums_ref in enumerate((own_ref, other_ref)):
        share = jnp.exp2(stat_ref[mine, 2 * side : 2 * side + 1, :] - top) / total
        for member in range(members):
            mass = None
            for head in range(heads):
                at = (member * heads + head) * rows
                term = sums_ref[:, at : at + rows] * share[:, at : at + rows]
                mass = term if mass is None else mass + term
            for run in range(mass_ref.shape[1]):
                mass_ref[member, run, side] = mass[run * 16 : run * 16 + 16, :]


def target_kernel(mass_ref, ws_ref, out_ref, lines_ref, *, devices, rows, heads):
    core = lax.axis_index("core")
    first = shard_of(lax.axis_index(PLACE), lax.axis_index("yl"), core) * rows
    place = first + lax.broadcasted_iota(jnp.int32, (1, rows), 1)
    visible = (place // BLOCK - ws_ref[...] // BLOCK + 1).astype(jnp.float32) * (1.0 / heads)
    for source in range(devices):
        for run in range(mass_ref.shape[1]):
            for side in range(2):
                begin = 2 * shard_of(run * 16, source // 2, core ^ side) + source % 2
                lines_ref[pl.ds(begin, 16, stride=4), :] = mass_ref[source, run, side] * visible
    out_ref[...] = lines_ref[...].T


GROUP = ("yl", "head")
PLACE = ("yh", "zh", "x")


def spread(x, axes):
    copies = jnp.broadcast_to(x[None], (lax.axis_size(axes), *x.shape))
    return lax.all_to_all(copies, axes, 0, 0, tiled=True)


def body(queries, keys, window_start):
    blocks = lax.axis_size(PLACE)
    devices = lax.axis_size(GROUP)
    members = devices // 2
    rows, heads_here, width = queries.shape
    heads = 2 * heads_here
    scale = 1.0 / math.sqrt(width)

    lines = jnp.transpose(queries, (2, 1, 0)).reshape(width, heads_here * rows)
    digits = jnp.stack([window_start // 256, window_start % 256]).astype(jnp.bfloat16)
    digits = jnp.pad(digits, ((0, 14), (0, (heads_here - 1) * rows)))
    lines = jnp.concatenate([lines, digits], axis=0)

    def trade(x, step):
        return lax.ppermute(x, GROUP, [(i, i ^ step) for i in range(devices)])

    own = lax.dynamic_slice_in_dim(keys, lax.axis_index("head") * BLOCK, BLOCK, 0)
    column, lines, near = lax.optimization_barrier((spread(spread(own, "zh"), "yh"), lines, trade(lines, 1)))
    own_keys = spread(column.reshape(-1, BLOCK, width), "x")
    across, along = trade(lines, 3), trade(lines, 2)
    all_queries = [lines, near, along, across]

    total_rows = members * heads * rows
    vmem = pl.BlockSpec(memory_space=pltpu.VMEM)
    params = pltpu.CompilerParams(vmem_limit_bytes=32 * 1024 * 1024)

    query_lines, starts, most = pl.pallas_call(
        functools.partial(prepare_kernel, scale=scale, rows=rows),
        out_shape=(
            jax.ShapeDtypeStruct((2 * width, total_rows), jnp.bfloat16),
            jax.ShapeDtypeStruct((devices, rows), jnp.int32),
            jax.ShapeDtypeStruct((8, rows), jnp.float32),
        ),
        in_specs=[vmem] * devices,
        out_specs=(vmem, vmem, vmem),
        compiler_params=params,
        cost_estimate=pl.CostEstimate(flops=10 * width * total_rows, bytes_accessed=2 * 1024 * 1024, transcendentals=0),
        name="prepare",
    )(*all_queries)

    own_keys, query_lines = lax.optimization_barrier((own_keys, query_lines))
    other_keys = lax.ppermute(own_keys, "core", [(0, 1), (1, 0)])

    def score(half_keys, swap):
        return pl.pallas_call(
            functools.partial(score_kernel, members=members, heads=heads, rows=rows, scale=scale, swap=swap),
            out_shape=(
                jax.ShapeDtypeStruct((blocks, total_rows), jnp.float32),
                jax.ShapeDtypeStruct((2, total_rows), jnp.float32),
            ),
            in_specs=[vmem] * 4,
            out_specs=(vmem, vmem),
            scratch_shapes=[
                pltpu.VMEM((members, CHUNK * BLOCK, rows), jnp.float32),
                pltpu.VMEM((2, CHUNK * BLOCK, 2 * rows), jnp.float32),
                pltpu.VMEM((total_rows // rows, CHUNK * 8, rows), jnp.float32),
                pltpu.VMEM((1, total_rows), jnp.float32),
            ],
            compiler_params=params,
            cost_estimate=pl.CostEstimate(
                flops=2 * blocks * BLOCK * width * total_rows,
                bytes_accessed=8 * 1024 * 1024,
                transcendentals=blocks * BLOCK * total_rows,
            ),
            name="score",
        )(most, starts, query_lines, half_keys)

    own_sums, own_stat = score(own_keys, 0)
    other_sums, other_stat = score(other_keys, 1)
    stats = spread(jnp.concatenate([own_stat, other_stat], axis=0), GROUP)
    mass = pl.pallas_call(
        functools.partial(mass_kernel, members=members, heads=heads, rows=rows),
        out_shape=jax.ShapeDtypeStruct((members, blocks // 16, 2, 16, rows), jnp.float32),
        in_specs=[vmem] * 3,
        out_specs=vmem,
        compiler_params=params,
        name="mass",
    )(own_sums, other_sums, stats)
    mass = mass.reshape(devices, blocks // 32, 2, 16, rows)
    mass = lax.all_to_all(mass, GROUP, 0, 0, tiled=True)
    return pl.pallas_call(
        functools.partial(target_kernel, devices=devices, rows=rows, heads=heads),
        out_shape=jax.ShapeDtypeStruct((rows, blocks * devices), jnp.float32),
        in_specs=[vmem] * 2,
        out_specs=vmem,
        scratch_shapes=[pltpu.VMEM((blocks * devices, rows), jnp.float32)],
        compiler_params=params,
        name="target",
    )(mass, window_start.reshape(1, rows))


def solution(mesh):
    grid = Mesh(mesh.devices.reshape(-1, 2, 4, 4, 2, 2), ("yh", "yl", "zh", "x", "core", "head"))
    seq = ("yh", "yl", "zh", "x", "core")
    placed = (P(seq, "head", None), P(seq, None), P(seq))
    return jax.shard_map(body, mesh=grid, in_specs=placed, out_specs=P(seq, "head"), check_vma=False)
```

```python
import functools
import math

import jax
import jax.numpy as jnp
import numpy as np
from jax import lax
from jax.experimental import pallas as pl
from jax.experimental.pallas import tpu as pltpu
from jax.sharding import Mesh, PartitionSpec as P

BLOCK = 64
CHUNK = 16
LOW = -1e30
SAFE = 60.0


def shard_of(index, low, core):
    return index // 16 * 64 + low * 32 + index % 16 * 2 + core


def prepare_kernel(*refs, scale, rows):
    *q_refs, lines_ref, starts_ref, most_ref = refs
    mine = lax.axis_index(GROUP)
    depth = lines_ref.shape[0] // 2
    half = lines_ref.shape[1] // len(q_refs)
    most = jnp.float32(0.0)
    for slot, q_ref in enumerate(q_refs):
        source = mine ^ slot
        raw = q_ref[0:depth, :].astype(jnp.float32)
        most = jnp.maximum(most, jnp.max(jnp.sum(raw * raw, axis=0, keepdims=True)))
        scaled = raw * scale
        high = scaled.astype(jnp.bfloat16)
        low = (scaled - high.astype(jnp.float32)).astype(jnp.bfloat16)
        at = pl.ds(pl.multiple_of(source * half, half), half)
        lines_ref[0:depth, at] = high
        lines_ref[depth : 2 * depth, at] = low
        digits = q_ref[depth : depth + 16, 0:rows].astype(jnp.float32)
        starts_ref[pl.ds(source, 1), :] = (digits[0:1, :] * 256.0 + digits[1:2, :]).astype(jnp.int32)
    most_ref[...] = jnp.full_like(most_ref, most)


def merge(first, second):
    top = jnp.maximum(first[0:1, :], second[0:1, :])
    total = first[1:2, :] * jnp.exp(first[0:1, :] - top) + second[1:2, :] * jnp.exp(second[0:1, :] - top)
    return top, total


def score_kernel(most_ref, starts_ref, lines_ref, keys_ref, *refs, members, heads, rows, scale, swap):
    if swap:
        earlier_ref, sums_ref, stat_ref, merged_ref, mask_ref, part_ref, top_ref = refs
    else:
        sums_ref, stat_ref, mask_ref, part_ref, top_ref = refs
    group = lax.axis_index(PLACE)
    mine = lax.axis_index(GROUP)
    core = lax.axis_index("core")
    side = core ^ swap
    span = CHUNK * BLOCK
    width = heads * rows
    pair = 2 * rows

    largest = jnp.max(jnp.abs(keys_ref[...]), axis=1).astype(jnp.float32)
    longest = jnp.max(jnp.sum(largest * largest, axis=-1))
    safe = jnp.max(most_ref[...]) * longest * (scale * scale) <= SAFE * SAFE
    sums_ref[...] = jnp.zeros_like(sums_ref)

    starts = [starts_ref[2 * member : 2 * member + 1, :] for member in range(members)]
    first_start = jnp.min(functools.reduce(jnp.minimum, starts))
    last_chunk = group // CHUNK
    first_chunk = jnp.minimum(first_start // (rows * 64), last_chunk)

    def chunk_keys(chunk):
        blocks = [keys_ref[column, chunk * 4 + step] for step in range(4) for column in range(4)]
        keys = jnp.concatenate(blocks, axis=0)
        return jnp.concatenate([keys, keys], axis=1)

    line = lax.broadcasted_iota(jnp.int32, (BLOCK, rows), 0)
    places = [
        shard_of(group, member, core) * rows + lax.broadcasted_iota(jnp.int32, (1, rows), 1) for member in range(members)
    ]

    def fill_mask(chunk, inside, outside):
        for block in range(CHUNK):
            base = (shard_of(chunk * CHUNK + block, mine // 2, side) * 2 + mine % 2) * BLOCK
            for member in range(members):
                allowed = (line >= starts[member] - base) & (line <= places[member] - base)
                mask_ref[member, block * BLOCK : (block + 1) * BLOCK, :] = jnp.where(allowed, inside, outside)

    def scores(keys, at):
        return jnp.dot(keys, lines_ref[:, pl.ds(at, pair)], preferred_element_type=jnp.float32)

    def lines_of(chunk):
        return pl.ds(pl.multiple_of(chunk * CHUNK, CHUNK), CHUNK)

    @pl.when(safe)
    def _():
        def one_chunk(chunk, carry):
            keys = chunk_keys(chunk)
            fill_mask(chunk, 1.0, 0.0)
            for tile in range(members * width // pair):
                at = tile * pair
                result = scores(keys, at)
                for block in range(CHUNK):
                    lines = slice(block * BLOCK, (block + 1) * BLOCK)
                    mask = mask_ref[at // width, lines, :]
                    for column in range(2):
                        x = result[lines, column * rows : (column + 1) * rows]
                        weights = jnp.exp(x) * mask
                        part_ref[2 * tile + column, block * 8 : block * 8 + 8, :] = jnp.sum(
                            weights.reshape(BLOCK // 8, 8, rows), axis=0
                        )
                for column in range(2):
                    total = part_ref[2 * tile + column, pl.ds(0, CHUNK, stride=8), :]
                    for line in range(1, 8):
                        total = total + part_ref[2 * tile + column, pl.ds(line, CHUNK, stride=8), :]
                    sums_ref[lines_of(chunk), at + column * rows : at + (column + 1) * rows] = total
            return carry

        lax.fori_loop(first_chunk, last_chunk + 1, one_chunk, 0)

    def each_tile(visit):
        def one_chunk(chunk, carry):
            fill_mask(chunk, 0.0, LOW)

            def one_tile(tile, carry):
                at = pl.multiple_of(tile * pair, pair)
                mask = mask_ref[at // width]
                visit(chunk, pl.ds(at, pair), scores(chunk_keys(chunk), at) + jnp.concatenate([mask, mask], axis=1))
                return carry

            return lax.fori_loop(0, members * width // pair, one_tile, carry)

        lax.fori_loop(first_chunk, last_chunk + 1, one_chunk, 0)

    @pl.when(jnp.logical_not(safe))
    def _():
        def raise_top(chunk, at, x):
            top_ref[:, at] = jnp.maximum(top_ref[:, at], jnp.max(x, axis=0, keepdims=True))

        def add(chunk, at, x):
            weights = jnp.where(x > 0.5 * LOW, jnp.exp(jnp.minimum(x - top_ref[:, at], 0.0)), 0.0)
            sums_ref[lines_of(chunk), at] = jnp.sum(weights.reshape(CHUNK, BLOCK, pair), axis=1)

        top_ref[...] = jnp.full_like(top_ref, LOW)
        each_tile(raise_top)
        each_tile(add)

    total = jnp.sum(sums_ref[...], axis=0, keepdims=True)
    top = jnp.where(safe, jnp.zeros_like(total), top_ref[...])
    stat_ref[0:1, :] = jnp.where(total > 0.0, top, LOW)
    stat_ref[1:2, :] = total
    if swap:
        merged_ref[0:1, :], merged_ref[1:2, :] = merge(stat_ref[...], earlier_ref[...])


def mass_kernel(own_ref, other_ref, own_stat_ref, other_stat_ref, stat_ref, mass_ref, *, members, heads, rows):
    top = jnp.max(stat_ref[:, 0, :], axis=0, keepdims=True)
    total = jnp.sum(stat_ref[:, 1, :] * jnp.exp(stat_ref[:, 0, :] - top), axis=0, keepdims=True)
    tops = (own_stat_ref[0:1, :], other_stat_ref[0:1, :])
    for side, sums_ref in enumerate((own_ref, other_ref)):
        share = jnp.exp(tops[side] - top) / total
        for member in range(members):
            mass = None
            for head in range(heads):
                at = (member * heads + head) * rows
                term = sums_ref[:, at : at + rows] * share[:, at : at + rows]
                mass = term if mass is None else mass + term
            for run in range(mass_ref.shape[1]):
                mass_ref[member, run, side] = mass[run * 16 : run * 16 + 16, :]


def target_kernel(mass_ref, ws_ref, out_ref, lines_ref, *, devices, rows, heads):
    core = lax.axis_index("core")
    first = shard_of(lax.axis_index(PLACE), lax.axis_index("yl"), core) * rows
    place = first + lax.broadcasted_iota(jnp.int32, (1, rows), 1)
    visible = (place // BLOCK - ws_ref[...] // BLOCK + 1).astype(jnp.float32) * (1.0 / heads)
    for source in range(devices):
        for run in range(mass_ref.shape[1]):
            for side in range(2):
                begin = 2 * shard_of(run * 16, source // 2, core ^ side) + source % 2
                lines_ref[pl.ds(begin, 16, stride=4), :] = mass_ref[source, run, side] * visible
    out_ref[...] = lines_ref[...].T


GROUP = ("yl", "head")
PLACE = ("yh", "zh", "x")


def spread(x, axes):
    copies = jnp.broadcast_to(x[None], (lax.axis_size(axes), *x.shape))
    return lax.all_to_all(copies, axes, 0, 0, tiled=True)


def body(queries, keys, window_start):
    blocks = lax.axis_size(PLACE)
    devices = lax.axis_size(GROUP)
    members = devices // 2
    rows, heads_here, width = queries.shape
    heads = 2 * heads_here
    scale = 1.0 / math.sqrt(width)

    lines = jnp.transpose(queries, (2, 1, 0)).reshape(width, heads_here * rows)
    digits = jnp.stack([window_start // 256, window_start % 256]).astype(jnp.bfloat16)
    digits = jnp.pad(digits, ((0, 14), (0, (heads_here - 1) * rows)))
    lines = jnp.concatenate([lines, digits], axis=0)

    def trade(x, step):
        return lax.ppermute(x, GROUP, [(i, i ^ step) for i in range(devices)])

    own = lax.dynamic_slice_in_dim(keys, lax.axis_index("head") * BLOCK, BLOCK, 0)
    column, lines, near = lax.optimization_barrier((spread(own, ("yh", "zh")), lines, trade(lines, 1)))
    own_keys = spread(column, "x")
    across, along = trade(lines, 3), trade(lines, 2)
    all_queries = [lines, near, along, across]

    total_rows = members * heads * rows
    vmem = pl.BlockSpec(memory_space=pltpu.VMEM)
    params = pltpu.CompilerParams(vmem_limit_bytes=32 * 1024 * 1024)

    query_lines, starts, most = pl.pallas_call(
        functools.partial(prepare_kernel, scale=scale, rows=rows),
        out_shape=(
            jax.ShapeDtypeStruct((2 * width, total_rows), jnp.bfloat16),
            jax.ShapeDtypeStruct((devices, rows), jnp.int32),
            jax.ShapeDtypeStruct((8, rows), jnp.float32),
        ),
        in_specs=[vmem] * devices,
        out_specs=(vmem, vmem, vmem),
        compiler_params=params,
        cost_estimate=pl.CostEstimate(flops=10 * width * total_rows, bytes_accessed=2 * 1024 * 1024, transcendentals=0),
        name="prepare",
    )(*all_queries)

    own_keys, query_lines = lax.optimization_barrier((own_keys, query_lines))
    other_keys = lax.ppermute(own_keys, "core", [(0, 1), (1, 0)])

    stat_shape = jax.ShapeDtypeStruct((2, total_rows), jnp.float32)

    def score(half_keys, *earlier):
        return pl.pallas_call(
            functools.partial(
                score_kernel, members=members, heads=heads, rows=rows, scale=scale, swap=len(earlier)
            ),
            out_shape=(jax.ShapeDtypeStruct((blocks, total_rows), jnp.float32), stat_shape) + (stat_shape,) * len(earlier),
            in_specs=[vmem] * (4 + len(earlier)),
            out_specs=(vmem,) * (2 + len(earlier)),
            scratch_shapes=[
                pltpu.VMEM((members, CHUNK * BLOCK, rows), jnp.float32),
                pltpu.VMEM((total_rows // rows, CHUNK * 8, rows), jnp.float32),
                pltpu.VMEM((1, total_rows), jnp.float32),
            ],
            compiler_params=params,
            cost_estimate=pl.CostEstimate(
                flops=2 * blocks * BLOCK * width * total_rows,
                bytes_accessed=8 * 1024 * 1024,
                transcendentals=blocks * BLOCK * total_rows,
            ),
            name="score",
        )(most, starts, query_lines, half_keys, *earlier)

    own_sums, own_stat = score(own_keys)
    other_sums, other_stat, stat = score(other_keys, own_stat)
    stats = spread(stat, GROUP)
    mass = pl.pallas_call(
        functools.partial(mass_kernel, members=members, heads=heads, rows=rows),
        out_shape=jax.ShapeDtypeStruct((members, blocks // 16, 2, 16, rows), jnp.float32),
        in_specs=[vmem] * 5,
        out_specs=vmem,
        compiler_params=params,
        name="mass",
    )(own_sums, other_sums, own_stat, other_stat, stats)
    mass = mass.reshape(devices, blocks // 32, 2, 16, rows)
    mass = lax.all_to_all(mass, GROUP, 0, 0, tiled=True)
    return pl.pallas_call(
        functools.partial(target_kernel, devices=devices, rows=rows, heads=heads),
        out_shape=jax.ShapeDtypeStruct((rows, blocks * devices), jnp.float32),
        in_specs=[vmem] * 2,
        out_specs=vmem,
        scratch_shapes=[pltpu.VMEM((blocks * devices, rows), jnp.float32)],
        compiler_params=params,
        name="target",
    )(mass, window_start.reshape(1, rows))


def solution(mesh):
    grid = Mesh(mesh.devices.reshape(-1, 2, 4, 4, 2, 2), ("yh", "yl", "zh", "x", "core", "head"))
    seq = ("yh", "yl", "zh", "x", "core")
    placed = (P(seq, "head", None), P(seq, None), P(seq))
    return jax.shard_map(body, mesh=grid, in_specs=placed, out_specs=P(seq, "head"), check_vma=False)
```

```python
import functools
import math

import jax
import jax.numpy as jnp
import numpy as np
from jax import lax
from jax.experimental import pallas as pl
from jax.experimental.pallas import tpu as pltpu
from jax.sharding import Mesh, PartitionSpec as P

BLOCK = 64
CHUNK = 16
LOW = -1e30
LOG2E = math.log2(math.e)
SAFE = 60.0


def shard_of(index, low, core):
    return index // 16 * 64 + low * 32 + index % 16 * 2 + core


def prepare_kernel(*refs, scale, rows):
    *q_refs, lines_ref, starts_ref, most_ref = refs
    mine = lax.axis_index(GROUP)
    depth = lines_ref.shape[0] // 2
    half = lines_ref.shape[1] // len(q_refs)
    most = jnp.float32(0.0)
    for slot, q_ref in enumerate(q_refs):
        source = mine ^ slot
        raw = q_ref[0:depth, :].astype(jnp.float32)
        most = jnp.maximum(most, jnp.max(jnp.sum(raw * raw, axis=0, keepdims=True)))
        scaled = raw * (scale * LOG2E)
        high = scaled.astype(jnp.bfloat16)
        low = (scaled - high.astype(jnp.float32)).astype(jnp.bfloat16)
        at = pl.ds(pl.multiple_of(source * half, half), half)
        lines_ref[0:depth, at] = high
        lines_ref[depth : 2 * depth, at] = low
        digits = q_ref[depth : depth + 16, 0:rows].astype(jnp.float32)
        starts_ref[pl.ds(source, 1), :] = (digits[0:1, :] * 256.0 + digits[1:2, :]).astype(jnp.int32)
    most_ref[...] = jnp.full_like(most_ref, most)


def merge(first, second):
    top = jnp.maximum(first[0:1, :], second[0:1, :])
    total = first[1:2, :] * jnp.exp2(first[0:1, :] - top) + second[1:2, :] * jnp.exp2(second[0:1, :] - top)
    return top, total


def score_kernel(most_ref, starts_ref, lines_ref, keys_ref, *refs, members, heads, rows, scale, swap):
    if swap:
        earlier_ref, sums_ref, stat_ref, merged_ref, mask_ref, part_ref, top_ref = refs
    else:
        sums_ref, stat_ref, mask_ref, part_ref, top_ref = refs
    group = lax.axis_index(PLACE)
    mine = lax.axis_index(GROUP)
    core = lax.axis_index("core")
    side = core ^ swap
    span = CHUNK * BLOCK
    width = heads * rows
    pair = 2 * rows

    largest = jnp.max(jnp.abs(keys_ref[...]), axis=1).astype(jnp.float32)
    longest = jnp.max(jnp.sum(largest * largest, axis=-1))
    safe = jnp.max(most_ref[...]) * longest * (scale * scale) <= SAFE * SAFE
    sums_ref[...] = jnp.zeros_like(sums_ref)

    starts = [starts_ref[2 * member : 2 * member + 1, :] for member in range(members)]
    first_start = jnp.min(functools.reduce(jnp.minimum, starts))
    last_chunk = group // CHUNK
    first_chunk = jnp.minimum(first_start // (rows * 64), last_chunk)

    def chunk_keys(chunk):
        blocks = [keys_ref[column, chunk * 4 + step] for step in range(4) for column in range(4)]
        keys = jnp.concatenate(blocks, axis=0)
        return jnp.concatenate([keys, keys], axis=1)

    line = lax.broadcasted_iota(jnp.int32, (BLOCK, rows), 0)
    places = [
        shard_of(group, member, core) * rows + lax.broadcasted_iota(jnp.int32, (1, rows), 1) for member in range(members)
    ]

    def fill_mask(chunk, inside, outside):
        for block in range(CHUNK):
            base = (shard_of(chunk * CHUNK + block, mine // 2, side) * 2 + mine % 2) * BLOCK
            for member in range(members):
                allowed = (line >= starts[member] - base) & (line <= places[member] - base)
                mask_ref[member, block * BLOCK : (block + 1) * BLOCK, :] = jnp.where(allowed, inside, outside)

    def scores(keys, at):
        return jnp.dot(keys, lines_ref[:, pl.ds(at, pair)], preferred_element_type=jnp.float32)

    def lines_of(chunk):
        return pl.ds(pl.multiple_of(chunk * CHUNK, CHUNK), CHUNK)

    @pl.when(safe)
    def _():
        def one_chunk(chunk, carry):
            keys = chunk_keys(chunk)
            fill_mask(chunk, 1.0, 0.0)
            for tile in range(members * width // pair):
                at = tile * pair
                result = scores(keys, at)
                for block in range(CHUNK):
                    lines = slice(block * BLOCK, (block + 1) * BLOCK)
                    mask = mask_ref[at // width, lines, :]
                    for column in range(2):
                        x = result[lines, column * rows : (column + 1) * rows]
                        weights = jnp.exp2(x) * mask
                        part_ref[2 * tile + column, block * 8 : block * 8 + 8, :] = jnp.sum(
                            weights.reshape(BLOCK // 8, 8, rows), axis=0
                        )
                for column in range(2):
                    total = part_ref[2 * tile + column, pl.ds(0, CHUNK, stride=8), :]
                    for line in range(1, 8):
                        total = total + part_ref[2 * tile + column, pl.ds(line, CHUNK, stride=8), :]
                    sums_ref[lines_of(chunk), at + column * rows : at + (column + 1) * rows] = total
            return carry

        lax.fori_loop(first_chunk, last_chunk + 1, one_chunk, 0)

    def each_tile(visit):
        def one_chunk(chunk, carry):
            fill_mask(chunk, 0.0, LOW)

            def one_tile(tile, carry):
                at = pl.multiple_of(tile * pair, pair)
                mask = mask_ref[at // width]
                visit(chunk, pl.ds(at, pair), scores(chunk_keys(chunk), at) + jnp.concatenate([mask, mask], axis=1))
                return carry

            return lax.fori_loop(0, members * width // pair, one_tile, carry)

        lax.fori_loop(first_chunk, last_chunk + 1, one_chunk, 0)

    @pl.when(jnp.logical_not(safe))
    def _():
        def raise_top(chunk, at, x):
            top_ref[:, at] = jnp.maximum(top_ref[:, at], jnp.max(x, axis=0, keepdims=True))

        def add(chunk, at, x):
            weights = jnp.where(x > 0.5 * LOW, jnp.exp2(jnp.minimum(x - top_ref[:, at], 0.0)), 0.0)
            sums_ref[lines_of(chunk), at] = jnp.sum(weights.reshape(CHUNK, BLOCK, pair), axis=1)

        top_ref[...] = jnp.full_like(top_ref, LOW)
        each_tile(raise_top)
        each_tile(add)

    total = jnp.sum(sums_ref[...], axis=0, keepdims=True)
    top = jnp.where(safe, jnp.zeros_like(total), top_ref[...])
    stat_ref[0:1, :] = jnp.where(total > 0.0, top, LOW)
    stat_ref[1:2, :] = total
    if swap:
        merged_ref[0:1, :], merged_ref[1:2, :] = merge(stat_ref[...], earlier_ref[...])


def mass_kernel(own_ref, other_ref, own_stat_ref, other_stat_ref, stat_ref, mass_ref, *, members, heads, rows):
    top = jnp.max(stat_ref[:, 0, :], axis=0, keepdims=True)
    total = jnp.sum(stat_ref[:, 1, :] * jnp.exp2(stat_ref[:, 0, :] - top), axis=0, keepdims=True)
    tops = (own_stat_ref[0:1, :], other_stat_ref[0:1, :])
    for side, sums_ref in enumerate((own_ref, other_ref)):
        share = jnp.exp2(tops[side] - top) / total
        for member in range(members):
            mass = None
            for head in range(heads):
                at = (member * heads + head) * rows
                term = sums_ref[:, at : at + rows] * share[:, at : at + rows]
                mass = term if mass is None else mass + term
            for run in range(mass_ref.shape[1]):
                mass_ref[member, run, side] = mass[run * 16 : run * 16 + 16, :]


def target_kernel(mass_ref, ws_ref, out_ref, lines_ref, *, devices, rows, heads):
    core = lax.axis_index("core")
    first = shard_of(lax.axis_index(PLACE), lax.axis_index("yl"), core) * rows
    place = first + lax.broadcasted_iota(jnp.int32, (1, rows), 1)
    visible = (place // BLOCK - ws_ref[...] // BLOCK + 1).astype(jnp.float32) * (1.0 / heads)
    for source in range(devices):
        for run in range(mass_ref.shape[1]):
            for side in range(2):
                begin = 2 * shard_of(run * 16, source // 2, core ^ side) + source % 2
                lines_ref[pl.ds(begin, 16, stride=4), :] = mass_ref[source, run, side] * visible
    out_ref[...] = lines_ref[...].T


GROUP = ("yl", "head")
PLACE = ("yh", "zh", "x")


def spread(x, axes):
    copies = jnp.broadcast_to(x[None], (lax.axis_size(axes), *x.shape))
    return lax.all_to_all(copies, axes, 0, 0, tiled=True)


def body(queries, keys, window_start):
    blocks = lax.axis_size(PLACE)
    devices = lax.axis_size(GROUP)
    members = devices // 2
    rows, heads_here, width = queries.shape
    heads = 2 * heads_here
    scale = 1.0 / math.sqrt(width)

    lines = jnp.transpose(queries, (2, 1, 0)).reshape(width, heads_here * rows)
    digits = jnp.stack([window_start // 256, window_start % 256]).astype(jnp.bfloat16)
    digits = jnp.pad(digits, ((0, 14), (0, (heads_here - 1) * rows)))
    lines = jnp.concatenate([lines, digits], axis=0)

    def trade(x, step):
        return lax.ppermute(x, GROUP, [(i, i ^ step) for i in range(devices)])

    own = lax.dynamic_slice_in_dim(keys, lax.axis_index("head") * BLOCK, BLOCK, 0)
    column, lines = lax.optimization_barrier((spread(own, ("yh", "zh")), lines))
    own_keys = spread(column, "x")
    all_queries = [lines, trade(lines, 1), trade(lines, 2), trade(lines, 3)]

    total_rows = members * heads * rows
    vmem = pl.BlockSpec(memory_space=pltpu.VMEM)
    params = pltpu.CompilerParams(vmem_limit_bytes=32 * 1024 * 1024)

    query_lines, starts, most = pl.pallas_call(
        functools.partial(prepare_kernel, scale=scale, rows=rows),
        out_shape=(
            jax.ShapeDtypeStruct((2 * width, total_rows), jnp.bfloat16),
            jax.ShapeDtypeStruct((devices, rows), jnp.int32),
            jax.ShapeDtypeStruct((8, rows), jnp.float32),
        ),
        in_specs=[vmem] * devices,
        out_specs=(vmem, vmem, vmem),
        compiler_params=params,
        cost_estimate=pl.CostEstimate(flops=10 * width * total_rows, bytes_accessed=2 * 1024 * 1024, transcendentals=0),
        name="prepare",
    )(*all_queries)

    own_keys, query_lines = lax.optimization_barrier((own_keys, query_lines))
    other_keys = lax.ppermute(own_keys, "core", [(0, 1), (1, 0)])

    stat_shape = jax.ShapeDtypeStruct((2, total_rows), jnp.float32)

    def score(half_keys, *earlier):
        return pl.pallas_call(
            functools.partial(
                score_kernel, members=members, heads=heads, rows=rows, scale=scale, swap=len(earlier)
            ),
            out_shape=(jax.ShapeDtypeStruct((blocks, total_rows), jnp.float32), stat_shape) + (stat_shape,) * len(earlier),
            in_specs=[vmem] * (4 + len(earlier)),
            out_specs=(vmem,) * (2 + len(earlier)),
            scratch_shapes=[
                pltpu.VMEM((members, CHUNK * BLOCK, rows), jnp.float32),
                pltpu.VMEM((total_rows // rows, CHUNK * 8, rows), jnp.float32),
                pltpu.VMEM((1, total_rows), jnp.float32),
            ],
            compiler_params=params,
            cost_estimate=pl.CostEstimate(
                flops=2 * blocks * BLOCK * width * total_rows,
                bytes_accessed=8 * 1024 * 1024,
                transcendentals=blocks * BLOCK * total_rows,
            ),
            name="score",
        )(most, starts, query_lines, half_keys, *earlier)

    own_sums, own_stat = score(own_keys)
    other_sums, other_stat, stat = score(other_keys, own_stat)
    stats = spread(stat, GROUP)
    mass = pl.pallas_call(
        functools.partial(mass_kernel, members=members, heads=heads, rows=rows),
        out_shape=jax.ShapeDtypeStruct((members, blocks // 16, 2, 16, rows), jnp.float32),
        in_specs=[vmem] * 5,
        out_specs=vmem,
        compiler_params=params,
        name="mass",
    )(own_sums, other_sums, own_stat, other_stat, stats)
    mass = mass.reshape(devices, blocks // 32, 2, 16, rows)
    mass = lax.all_to_all(mass, GROUP, 0, 0, tiled=True)
    return pl.pallas_call(
        functools.partial(target_kernel, devices=devices, rows=rows, heads=heads),
        out_shape=jax.ShapeDtypeStruct((rows, blocks * devices), jnp.float32),
        in_specs=[vmem] * 2,
        out_specs=vmem,
        scratch_shapes=[pltpu.VMEM((blocks * devices, rows), jnp.float32)],
        compiler_params=params,
        name="target",
    )(mass, window_start.reshape(1, rows))


def solution(mesh):
    grid = Mesh(mesh.devices.reshape(-1, 2, 4, 4, 2, 2), ("yh", "yl", "zh", "x", "core", "head"))
    seq = ("yh", "yl", "zh", "x", "core")
    placed = (P(seq, "head", None), P(seq, None), P(seq))
    return jax.shard_map(body, mesh=grid, in_specs=placed, out_specs=P(seq, "head"), check_vma=False)
```

```python
import functools
import math

import jax
import jax.numpy as jnp
import numpy as np
from jax import lax
from jax.experimental import pallas as pl
from jax.experimental.pallas import tpu as pltpu
from jax.sharding import Mesh, PartitionSpec as P

BLOCK = 64
CHUNK = 16
LOW = -1e30
LOG2E = math.log2(math.e)
SAFE = 60.0


def shard_of(index, low, core):
    return index // 16 * 64 + low * 32 + index % 16 * 2 + core


def prepare_kernel(*refs, scale, rows, heads):
    *q_refs, lines_ref, starts_ref, places_ref, order_ref, most_ref, raw_ref, aux_ref = refs
    mine = lax.axis_index(GROUP)
    depth = lines_ref.shape[0] // 2
    total = 2 * rows
    most = jnp.float32(0.0)
    for slot, q_ref in enumerate(q_refs):
        source = mine ^ slot
        raw = q_ref[0:depth, :]
        wide = raw.astype(jnp.float32)
        most = jnp.maximum(most, jnp.max(jnp.sum(wide * wide, axis=0, keepdims=True)))
        raw_ref[source] = raw
        aux_ref[source] = q_ref[depth : depth + 16, 0:rows]
    most_ref[...] = jnp.full_like(most_ref, most)

    aux = jnp.concatenate([aux_ref[0], aux_ref[2]], axis=1).astype(jnp.float32)
    row = lax.broadcasted_iota(jnp.int32, (1, total), 1).astype(jnp.float32)
    start = aux[0:1, :] * 256.0 + aux[1:2, :]
    key = jnp.broadcast_to(start * float(total) + row, (total, total))
    rank = jnp.sum(jnp.where(key.T < key, 1.0, 0.0), axis=0, keepdims=True)
    line = lax.broadcasted_iota(jnp.int32, (total, total), 0).astype(jnp.float32)
    order = jnp.where(rank == line, 1.0, 0.0).astype(jnp.bfloat16)
    order_ref[...] = order

    def in_order(values):
        return lax.dot_general(values, order, (((1,), (1,)), ((), ())), preferred_element_type=jnp.float32)

    spots = in_order(jnp.where(lax.broadcasted_iota(jnp.int32, aux.shape, 0) == 2, row, aux).astype(jnp.bfloat16))
    group = lax.axis_index(PLACE)
    core = lax.axis_index("core")
    for half in range(2):
        here = spots[:, half * rows : (half + 1) * rows]
        index = here[2:3, :].astype(jnp.int32)
        starts_ref[half : half + 1, :] = (here[0:1, :] * 256.0 + here[1:2, :]).astype(jnp.int32)
        places_ref[half : half + 1, :] = shard_of(group, index // rows, core) * rows + index % rows

    for head in range(heads):
        source = head // 4
        lane = slice(head % 4 * rows, (head % 4 + 1) * rows)
        x = in_order(jnp.concatenate([raw_ref[source, :, lane], raw_ref[2 + source, :, lane]], axis=1))
        x = x * (scale * LOG2E)
        high = x.astype(jnp.bfloat16)
        low = (x - high.astype(jnp.float32)).astype(jnp.bfloat16)
        for half in range(2):
            at = slice((half * heads + head) * rows, (half * heads + head + 1) * rows)
            lines_ref[0:depth, at] = high[:, half * rows : (half + 1) * rows]
            lines_ref[depth : 2 * depth, at] = low[:, half * rows : (half + 1) * rows]


def merge(first, second):
    top = jnp.maximum(first[0:1, :], second[0:1, :])
    total = first[1:2, :] * jnp.exp2(first[0:1, :] - top) + second[1:2, :] * jnp.exp2(second[0:1, :] - top)
    return top, total


def score_kernel(most_ref, starts_ref, places_ref, lines_ref, keys_ref, *refs, members, heads, rows, scale, swap):
    if swap:
        earlier_ref, sums_ref, stat_ref, merged_ref, mask_ref, part_ref, top_ref = refs
    else:
        sums_ref, stat_ref, mask_ref, part_ref, top_ref = refs
    group = lax.axis_index(PLACE)
    mine = lax.axis_index(GROUP)
    core = lax.axis_index("core")
    side = core ^ swap
    span = CHUNK * BLOCK
    width = heads * rows
    pair = 2 * rows

    largest = jnp.max(jnp.abs(keys_ref[...]), axis=1).astype(jnp.float32)
    longest = jnp.max(jnp.sum(largest * largest, axis=-1))
    safe = jnp.max(most_ref[...]) * longest * (scale * scale) <= SAFE * SAFE
    sums_ref[...] = jnp.zeros_like(sums_ref)

    reach = rows * 32
    parity = mine // 2
    last_chunk = group // CHUNK
    starts = [starts_ref[half : half + 1, :] for half in range(members)]
    places = [places_ref[half : half + 1, :] for half in range(members)]
    first_chunks = [(starts_ref[half, 0] // reach - parity + 1) // 2 for half in range(members)]

    def chunk_keys(chunk):
        blocks = [keys_ref[column, chunk * 4 + step] for step in range(4) for column in range(4)]
        keys = jnp.concatenate(blocks, axis=0)
        return jnp.concatenate([keys, keys], axis=1)

    line = lax.broadcasted_iota(jnp.int32, (BLOCK, rows), 0)

    def fill_mask(chunk, half, inside, outside):
        for block in range(CHUNK):
            base = (shard_of(chunk * CHUNK + block, parity, side) * 2 + mine % 2) * BLOCK
            allowed = (line >= starts[half] - base) & (line <= places[half] - base)
            mask_ref[half, block * BLOCK : (block + 1) * BLOCK, :] = jnp.where(allowed, inside, outside)

    def scores(keys, at):
        return jnp.dot(keys, lines_ref[:, pl.ds(at, pair)], preferred_element_type=jnp.float32)

    def lines_of(chunk):
        return pl.ds(pl.multiple_of(chunk * CHUNK, CHUNK), CHUNK)

    def each_chunk(half, visit):
        lax.fori_loop(first_chunks[half], last_chunk + 1, visit, 0)

    def some_tiles(half):
        def one_chunk(chunk, carry):
            keys = chunk_keys(chunk)
            fill_mask(chunk, half, 1.0, 0.0)
            for tile in range(half * width // pair, (half + 1) * width // pair):
                at = tile * pair
                result = scores(keys, at)
                for block in range(CHUNK):
                    lines = slice(block * BLOCK, (block + 1) * BLOCK)
                    mask = mask_ref[half, lines, :]
                    for column in range(2):
                        x = result[lines, column * rows : (column + 1) * rows]
                        weights = jnp.exp2(x) * mask
                        part_ref[2 * tile + column, block * 8 : block * 8 + 8, :] = jnp.sum(
                            weights.reshape(BLOCK // 8, 8, rows), axis=0
                        )
                for column in range(2):
                    total = part_ref[2 * tile + column, pl.ds(0, CHUNK, stride=8), :]
                    for line in range(1, 8):
                        total = total + part_ref[2 * tile + column, pl.ds(line, CHUNK, stride=8), :]
                    sums_ref[lines_of(chunk), at + column * rows : at + (column + 1) * rows] = total
            return carry

        each_chunk(half, one_chunk)

    @pl.when(safe)
    def _():
        for half in range(members):
            some_tiles(half)

    def each_tile(half, visit):
        def one_chunk(chunk, carry):
            fill_mask(chunk, half, 0.0, LOW)

            def one_tile(tile, carry):
                at = pl.multiple_of(half * width + tile * pair, pair)
                mask = mask_ref[half]
                visit(chunk, pl.ds(at, pair), scores(chunk_keys(chunk), at) + jnp.concatenate([mask, mask], axis=1))
                return carry

            return lax.fori_loop(0, width // pair, one_tile, carry)

        each_chunk(half, one_chunk)

    @pl.when(jnp.logical_not(safe))
    def _():
        def raise_top(chunk, at, x):
            top_ref[:, at] = jnp.maximum(top_ref[:, at], jnp.max(x, axis=0, keepdims=True))

        def add(chunk, at, x):
            weights = jnp.where(x > 0.5 * LOW, jnp.exp2(jnp.minimum(x - top_ref[:, at], 0.0)), 0.0)
            sums_ref[lines_of(chunk), at] = jnp.sum(weights.reshape(CHUNK, BLOCK, pair), axis=1)

        top_ref[...] = jnp.full_like(top_ref, LOW)
        for half in range(members):
            each_tile(half, raise_top)
            each_tile(half, add)

    total = jnp.sum(sums_ref[...], axis=0, keepdims=True)
    top = jnp.where(safe, jnp.zeros_like(total), top_ref[...])
    stat_ref[0:1, :] = jnp.where(total > 0.0, top, LOW)
    stat_ref[1:2, :] = total
    if swap:
        merged_ref[0:1, :], merged_ref[1:2, :] = merge(stat_ref[...], earlier_ref[...])


def mass_kernel(own_ref, other_ref, own_stat_ref, other_stat_ref, stat_ref, order_ref, mass_ref, *, members, heads, rows):
    top = jnp.max(stat_ref[:, 0, :], axis=0, keepdims=True)
    total = jnp.sum(stat_ref[:, 1, :] * jnp.exp2(stat_ref[:, 0, :] - top), axis=0, keepdims=True)
    tops = (own_stat_ref[0:1, :], other_stat_ref[0:1, :])
    order = order_ref[...]
    for side, sums_ref in enumerate((own_ref, other_ref)):
        share = jnp.exp2(tops[side] - top) / total
        halves = []
        for half in range(members):
            mass = None
            for head in range(heads):
                at = (half * heads + head) * rows
                term = sums_ref[:, at : at + rows] * share[:, at : at + rows]
                mass = term if mass is None else mass + term
            halves.append(mass)
        rest = jnp.concatenate(halves, axis=1)
        mass = None
        for _ in range(3):
            term = rest.astype(jnp.bfloat16)
            rest = rest - term.astype(jnp.float32)
            back = jnp.dot(term, order, preferred_element_type=jnp.float32)
            mass = back if mass is None else mass + back
        for member in range(members):
            for level in range(mass_ref.shape[1]):
                mass_ref[member, level, side] = mass[level * 16 : level * 16 + 16, member * rows : (member + 1) * rows]


def target_kernel(mass_ref, ws_ref, out_ref, lines_ref, *, devices, rows, heads):
    core = lax.axis_index("core")
    first = shard_of(lax.axis_index(PLACE), lax.axis_index("yl"), core) * rows
    place = first + lax.broadcasted_iota(jnp.int32, (1, rows), 1)
    visible = (place // BLOCK - ws_ref[...] // BLOCK + 1).astype(jnp.float32) * (1.0 / heads)
    for source in range(devices):
        for run in range(mass_ref.shape[1]):
            for side in range(2):
                begin = 2 * shard_of(run * 16, source // 2, core ^ side) + source % 2
                lines_ref[pl.ds(begin, 16, stride=4), :] = mass_ref[source, run, side] * visible
    out_ref[...] = lines_ref[...].T


GROUP = ("yl", "head")
PLACE = ("yh", "zh", "x")


def spread(x, axes):
    copies = jnp.broadcast_to(x[None], (lax.axis_size(axes), *x.shape))
    return lax.all_to_all(copies, axes, 0, 0, tiled=True)


def body(queries, keys, window_start):
    blocks = lax.axis_size(PLACE)
    devices = lax.axis_size(GROUP)
    members = devices // 2
    rows, heads_here, width = queries.shape
    heads = 2 * heads_here
    scale = 1.0 / math.sqrt(width)

    lines = jnp.transpose(queries, (2, 1, 0)).reshape(width, heads_here * rows)
    digits = jnp.stack([window_start // 256, window_start % 256]).astype(jnp.bfloat16)
    digits = jnp.pad(digits, ((0, 14), (0, (heads_here - 1) * rows)))
    lines = jnp.concatenate([lines, digits], axis=0)

    def trade(x, step):
        return lax.ppermute(x, GROUP, [(i, i ^ step) for i in range(devices)])

    own = lax.dynamic_slice_in_dim(keys, lax.axis_index("head") * BLOCK, BLOCK, 0)
    column, lines = lax.optimization_barrier((spread(own, ("yh", "zh")), lines))
    own_keys = spread(column, "x")
    all_queries = [lines, trade(lines, 1), trade(lines, 2), trade(lines, 3)]

    total_rows = members * heads * rows
    vmem = pl.BlockSpec(memory_space=pltpu.VMEM)
    params = pltpu.CompilerParams(vmem_limit_bytes=32 * 1024 * 1024)

    query_lines, starts, places, order, most = pl.pallas_call(
        functools.partial(prepare_kernel, scale=scale, rows=rows, heads=heads),
        out_shape=(
            jax.ShapeDtypeStruct((2 * width, total_rows), jnp.bfloat16),
            jax.ShapeDtypeStruct((members, rows), jnp.int32),
            jax.ShapeDtypeStruct((members, rows), jnp.int32),
            jax.ShapeDtypeStruct((members * rows, members * rows), jnp.bfloat16),
            jax.ShapeDtypeStruct((8, rows), jnp.float32),
        ),
        in_specs=[vmem] * devices,
        out_specs=(vmem,) * 5,
        scratch_shapes=[
            pltpu.VMEM((devices, width, heads_here * rows), jnp.bfloat16),
            pltpu.VMEM((devices, 16, rows), jnp.bfloat16),
        ],
        compiler_params=params,
        cost_estimate=pl.CostEstimate(flops=20 * width * total_rows, bytes_accessed=2 * 1024 * 1024, transcendentals=0),
        name="prepare",
    )(*all_queries)

    own_keys, query_lines = lax.optimization_barrier((own_keys, query_lines))
    other_keys = lax.ppermute(own_keys, "core", [(0, 1), (1, 0)])

    stat_shape = jax.ShapeDtypeStruct((2, total_rows), jnp.float32)

    def score(half_keys, *earlier):
        return pl.pallas_call(
            functools.partial(
                score_kernel, members=members, heads=heads, rows=rows, scale=scale, swap=len(earlier)
            ),
            out_shape=(jax.ShapeDtypeStruct((blocks, total_rows), jnp.float32), stat_shape) + (stat_shape,) * len(earlier),
            in_specs=[vmem] * (5 + len(earlier)),
            out_specs=(vmem,) * (2 + len(earlier)),
            scratch_shapes=[
                pltpu.VMEM((members, CHUNK * BLOCK, rows), jnp.float32),
                pltpu.VMEM((total_rows // rows, CHUNK * 8, rows), jnp.float32),
                pltpu.VMEM((1, total_rows), jnp.float32),
            ],
            compiler_params=params,
            cost_estimate=pl.CostEstimate(
                flops=2 * blocks * BLOCK * width * total_rows,
                bytes_accessed=8 * 1024 * 1024,
                transcendentals=blocks * BLOCK * total_rows,
            ),
            name="score",
        )(most, starts, places, query_lines, half_keys, *earlier)

    own_sums, own_stat = score(own_keys)
    other_sums, other_stat, stat = score(other_keys, own_stat)
    stats = spread(stat, GROUP)
    mass = pl.pallas_call(
        functools.partial(mass_kernel, members=members, heads=heads, rows=rows),
        out_shape=jax.ShapeDtypeStruct((members, blocks // 16, 2, 16, rows), jnp.float32),
        in_specs=[vmem] * 6,
        out_specs=vmem,
        compiler_params=params,
        name="mass",
    )(own_sums, other_sums, own_stat, other_stat, stats, order)
    mass = mass.reshape(devices, blocks // 32, 2, 16, rows)
    mass = lax.all_to_all(mass, GROUP, 0, 0, tiled=True)
    return pl.pallas_call(
        functools.partial(target_kernel, devices=devices, rows=rows, heads=heads),
        out_shape=jax.ShapeDtypeStruct((rows, blocks * devices), jnp.float32),
        in_specs=[vmem] * 2,
        out_specs=vmem,
        scratch_shapes=[pltpu.VMEM((blocks * devices, rows), jnp.float32)],
        compiler_params=params,
        name="target",
    )(mass, window_start.reshape(1, rows))


def solution(mesh):
    grid = Mesh(mesh.devices.reshape(-1, 2, 4, 4, 2, 2), ("yh", "yl", "zh", "x", "core", "head"))
    seq = ("yh", "yl", "zh", "x", "core")
    placed = (P(seq, "head", None), P(seq, None), P(seq))
    return jax.shard_map(body, mesh=grid, in_specs=placed, out_specs=P(seq, "head"), check_vma=False)
```

```python
import functools
import math

import jax
import jax.numpy as jnp
import numpy as np
from jax import lax
from jax.experimental import pallas as pl
from jax.experimental.pallas import tpu as pltpu
from jax.sharding import Mesh, PartitionSpec as P

BLOCK = 64
CHUNK = 16
LOW = -1e30
LOG2E = math.log2(math.e)
SAFE = 60.0


def shard_of(index, low, core):
    return index // 16 * 64 + low * 32 + index % 16 * 2 + core


def prepare_kernel(*refs, scale, rows):
    *q_refs, lines_ref, starts_ref, most_ref = refs
    mine = lax.axis_index(GROUP)
    depth = lines_ref.shape[0] // 2
    half = lines_ref.shape[1] // len(q_refs)
    most = jnp.float32(0.0)
    for slot, q_ref in enumerate(q_refs):
        source = mine ^ slot
        raw = q_ref[0:depth, :].astype(jnp.float32)
        most = jnp.maximum(most, jnp.max(jnp.sum(raw * raw, axis=0, keepdims=True)))
        scaled = raw * (scale * LOG2E)
        high = scaled.astype(jnp.bfloat16)
        low = (scaled - high.astype(jnp.float32)).astype(jnp.bfloat16)
        at = pl.ds(pl.multiple_of(source * half, half), half)
        lines_ref[0:depth, at] = high
        lines_ref[depth : 2 * depth, at] = low
        digits = q_ref[depth : depth + 16, 0:rows].astype(jnp.float32)
        starts_ref[pl.ds(source, 1), :] = (digits[0:1, :] * 256.0 + digits[1:2, :]).astype(jnp.int32)
    most_ref[...] = jnp.full_like(most_ref, most)


def merge(first, second):
    top = jnp.maximum(first[0:1, :], second[0:1, :])
    total = first[1:2, :] * jnp.exp2(first[0:1, :] - top) + second[1:2, :] * jnp.exp2(second[0:1, :] - top)
    return top, total


def score_kernel(most_ref, starts_ref, lines_ref, keys_ref, *refs, members, heads, rows, scale, swap):
    if swap:
        earlier_ref, sums_ref, stat_ref, merged_ref, mask_ref, part_ref, top_ref = refs
    else:
        sums_ref, stat_ref, mask_ref, part_ref, top_ref = refs
    group = lax.axis_index(PLACE)
    mine = lax.axis_index(GROUP)
    core = lax.axis_index("core")
    side = core ^ swap
    span = CHUNK * BLOCK
    width = heads * rows
    pair = 2 * rows

    largest = jnp.max(jnp.abs(keys_ref[...]), axis=1).astype(jnp.float32)
    longest = jnp.max(jnp.sum(largest * largest, axis=-1))
    safe = jnp.max(most_ref[...]) * longest * (scale * scale) <= SAFE * SAFE
    sums_ref[...] = jnp.zeros_like(sums_ref)

    starts = [starts_ref[2 * member : 2 * member + 1, :] for member in range(members)]
    first_start = jnp.min(functools.reduce(jnp.minimum, starts))
    last_chunk = group // CHUNK
    first_chunk = jnp.minimum(first_start // (rows * 64), last_chunk)

    def chunk_keys(chunk):
        blocks = [keys_ref[column, chunk * 4 + step] for step in range(4) for column in range(4)]
        keys = jnp.concatenate(blocks, axis=0)
        return jnp.concatenate([keys, keys], axis=1)

    line = lax.broadcasted_iota(jnp.int32, (BLOCK, rows), 0)
    places = [
        shard_of(group, member, core) * rows + lax.broadcasted_iota(jnp.int32, (1, rows), 1) for member in range(members)
    ]

    def fill_mask(chunk, inside, outside):
        for block in range(CHUNK):
            base = (shard_of(chunk * CHUNK + block, mine // 2, side) * 2 + mine % 2) * BLOCK
            for member in range(members):
                allowed = (line >= starts[member] - base) & (line <= places[member] - base)
                mask_ref[member, block * BLOCK : (block + 1) * BLOCK, :] = jnp.where(allowed, inside, outside)

    def scores(keys, at):
        return jnp.dot(keys, lines_ref[:, pl.ds(at, pair)], preferred_element_type=jnp.float32)

    def lines_of(chunk):
        return pl.ds(pl.multiple_of(chunk * CHUNK, CHUNK), CHUNK)

    @pl.when(safe)
    def _():
        def one_chunk(chunk, carry):
            keys = chunk_keys(chunk)
            fill_mask(chunk, 1.0, 0.0)
            for tile in range(members * width // pair):
                at = tile * pair
                result = scores(keys, at)
                for block in range(CHUNK):
                    lines = slice(block * BLOCK, (block + 1) * BLOCK)
                    mask = mask_ref[at // width, lines, :]
                    for column in range(2):
                        x = result[lines, column * rows : (column + 1) * rows]
                        weights = jnp.exp2(x) * mask
                        part_ref[2 * tile + column, block * 8 : block * 8 + 8, :] = jnp.sum(
                            weights.reshape(BLOCK // 8, 8, rows), axis=0
                        )
                for column in range(2):
                    total = part_ref[2 * tile + column, pl.ds(0, CHUNK, stride=8), :]
                    for line in range(1, 8):
                        total = total + part_ref[2 * tile + column, pl.ds(line, CHUNK, stride=8), :]
                    sums_ref[lines_of(chunk), at + column * rows : at + (column + 1) * rows] = total
            return carry

        lax.fori_loop(first_chunk, last_chunk + 1, one_chunk, 0)

    def each_tile(visit):
        def one_chunk(chunk, carry):
            fill_mask(chunk, 0.0, LOW)

            def one_tile(tile, carry):
                at = pl.multiple_of(tile * pair, pair)
                mask = mask_ref[at // width]
                visit(chunk, pl.ds(at, pair), scores(chunk_keys(chunk), at) + jnp.concatenate([mask, mask], axis=1))
                return carry

            return lax.fori_loop(0, members * width // pair, one_tile, carry)

        lax.fori_loop(first_chunk, last_chunk + 1, one_chunk, 0)

    @pl.when(jnp.logical_not(safe))
    def _():
        def raise_top(chunk, at, x):
            top_ref[:, at] = jnp.maximum(top_ref[:, at], jnp.max(x, axis=0, keepdims=True))

        def add(chunk, at, x):
            weights = jnp.where(x > 0.5 * LOW, jnp.exp2(jnp.minimum(x - top_ref[:, at], 0.0)), 0.0)
            sums_ref[lines_of(chunk), at] = jnp.sum(weights.reshape(CHUNK, BLOCK, pair), axis=1)

        top_ref[...] = jnp.full_like(top_ref, LOW)
        each_tile(raise_top)
        each_tile(add)

    total = jnp.sum(sums_ref[...], axis=0, keepdims=True)
    top = jnp.where(safe, jnp.zeros_like(total), top_ref[...])
    stat_ref[0:1, :] = jnp.where(total > 0.0, top, LOW)
    stat_ref[1:2, :] = total
    if swap:
        merged_ref[0:1, :], merged_ref[1:2, :] = merge(stat_ref[...], earlier_ref[...])


def mass_kernel(own_ref, other_ref, own_stat_ref, other_stat_ref, stat_ref, mass_ref, *, members, heads, rows):
    top = jnp.max(stat_ref[:, 0, :], axis=0, keepdims=True)
    total = jnp.sum(stat_ref[:, 1, :] * jnp.exp2(stat_ref[:, 0, :] - top), axis=0, keepdims=True)
    tops = (own_stat_ref[0:1, :], other_stat_ref[0:1, :])
    for side, sums_ref in enumerate((own_ref, other_ref)):
        share = jnp.exp2(tops[side] - top) / total
        for member in range(members):
            mass = None
            for head in range(heads):
                at = (member * heads + head) * rows
                term = sums_ref[:, at : at + rows] * share[:, at : at + rows]
                mass = term if mass is None else mass + term
            for run in range(mass_ref.shape[1]):
                mass_ref[member, run, side] = mass[run * 16 : run * 16 + 16, :]


def target_kernel(mass_ref, ws_ref, out_ref, lines_ref, *, devices, rows, heads):
    core = lax.axis_index("core")
    first = shard_of(lax.axis_index(PLACE), lax.axis_index("yl"), core) * rows
    place = first + lax.broadcasted_iota(jnp.int32, (1, rows), 1)
    visible = (place // BLOCK - ws_ref[...] // BLOCK + 1).astype(jnp.float32) * (1.0 / heads)
    for source in range(devices):
        for run in range(mass_ref.shape[1]):
            for side in range(2):
                begin = 2 * shard_of(run * 16, source // 2, core ^ side) + source % 2
                lines_ref[pl.ds(begin, 16, stride=4), :] = mass_ref[source, run, side] * visible
    out_ref[...] = lines_ref[...].T


GROUP = ("yl", "head")
PLACE = ("yh", "zh", "x")


def spread(x, axes):
    copies = jnp.broadcast_to(x[None], (lax.axis_size(axes), *x.shape))
    return lax.all_to_all(copies, axes, 0, 0, tiled=True)


def body(queries, keys, window_start):
    blocks = lax.axis_size(PLACE)
    devices = lax.axis_size(GROUP)
    members = devices // 2
    rows, heads_here, width = queries.shape
    heads = 2 * heads_here
    scale = 1.0 / math.sqrt(width)

    lines = jnp.transpose(queries, (2, 1, 0)).reshape(width, heads_here * rows)
    digits = jnp.stack([window_start // 256, window_start % 256]).astype(jnp.bfloat16)
    digits = jnp.pad(digits, ((0, 14), (0, (heads_here - 1) * rows)))
    lines = jnp.concatenate([lines, digits], axis=0)

    def trade(x, step):
        return lax.ppermute(x, GROUP, [(i, i ^ step) for i in range(devices)])

    own = lax.dynamic_slice_in_dim(keys, lax.axis_index("head") * BLOCK, BLOCK, 0)
    column, lines, near = lax.optimization_barrier((spread(own, ("yh", "zh")), lines, trade(lines, 1)))
    own_keys = spread(column, "x")
    across, along = trade(lines, 3), trade(lines, 2)
    all_queries = [lines, near, along, across]

    total_rows = members * heads * rows
    vmem = pl.BlockSpec(memory_space=pltpu.VMEM)
    params = pltpu.CompilerParams(vmem_limit_bytes=32 * 1024 * 1024)

    query_lines, starts, most = pl.pallas_call(
        functools.partial(prepare_kernel, scale=scale, rows=rows),
        out_shape=(
            jax.ShapeDtypeStruct((2 * width, total_rows), jnp.bfloat16),
            jax.ShapeDtypeStruct((devices, rows), jnp.int32),
            jax.ShapeDtypeStruct((8, rows), jnp.float32),
        ),
        in_specs=[vmem] * devices,
        out_specs=(vmem, vmem, vmem),
        compiler_params=params,
        cost_estimate=pl.CostEstimate(flops=10 * width * total_rows, bytes_accessed=2 * 1024 * 1024, transcendentals=0),
        name="prepare",
    )(*all_queries)

    own_keys, query_lines = lax.optimization_barrier((own_keys, query_lines))
    other_keys = lax.ppermute(own_keys, "core", [(0, 1), (1, 0)])

    stat_shape = jax.ShapeDtypeStruct((2, total_rows), jnp.float32)

    def score(half_keys, *earlier):
        return pl.pallas_call(
            functools.partial(
                score_kernel, members=members, heads=heads, rows=rows, scale=scale, swap=len(earlier)
            ),
            out_shape=(jax.ShapeDtypeStruct((blocks, total_rows), jnp.float32), stat_shape) + (stat_shape,) * len(earlier),
            in_specs=[vmem] * (4 + len(earlier)),
            out_specs=(vmem,) * (2 + len(earlier)),
            scratch_shapes=[
                pltpu.VMEM((members, CHUNK * BLOCK, rows), jnp.float32),
                pltpu.VMEM((total_rows // rows, CHUNK * 8, rows), jnp.float32),
                pltpu.VMEM((1, total_rows), jnp.float32),
            ],
            compiler_params=params,
            cost_estimate=pl.CostEstimate(
                flops=2 * blocks * BLOCK * width * total_rows,
                bytes_accessed=8 * 1024 * 1024,
                transcendentals=blocks * BLOCK * total_rows,
            ),
            name="score",
        )(most, starts, query_lines, half_keys, *earlier)

    own_sums, own_stat = score(own_keys)
    other_sums, other_stat, stat = score(other_keys, own_stat)
    stats = spread(stat, GROUP)
    mass = pl.pallas_call(
        functools.partial(mass_kernel, members=members, heads=heads, rows=rows),
        out_shape=jax.ShapeDtypeStruct((members, blocks // 16, 2, 16, rows), jnp.float32),
        in_specs=[vmem] * 5,
        out_specs=vmem,
        compiler_params=params,
        name="mass",
    )(own_sums, other_sums, own_stat, other_stat, stats)
    mass = mass.reshape(devices, blocks // 32, 2, 16, rows)
    mass = lax.all_to_all(mass, GROUP, 0, 0, tiled=True)
    return pl.pallas_call(
        functools.partial(target_kernel, devices=devices, rows=rows, heads=heads),
        out_shape=jax.ShapeDtypeStruct((rows, blocks * devices), jnp.float32),
        in_specs=[vmem] * 2,
        out_specs=vmem,
        scratch_shapes=[pltpu.VMEM((blocks * devices, rows), jnp.float32)],
        compiler_params=params,
        name="target",
    )(mass, window_start.reshape(1, rows))


def solution(mesh):
    grid = Mesh(mesh.devices.reshape(-1, 2, 4, 4, 2, 2), ("yh", "yl", "zh", "x", "core", "head"))
    seq = ("yh", "yl", "zh", "x", "core")
    placed = (P(seq, "head", None), P(seq, None), P(seq))
    return jax.shard_map(body, mesh=grid, in_specs=placed, out_specs=P(seq, "head"), check_vma=False)
```

```python
import functools
import math

import jax
import jax.numpy as jnp
import numpy as np
from jax import lax
from jax.experimental import pallas as pl
from jax.experimental.pallas import tpu as pltpu
from jax.sharding import Mesh, PartitionSpec as P

BLOCK = 64
CHUNK = 16
LOW = -1e30
LOG2E = math.log2(math.e)
SAFE = 60.0


def shard_of(index, low, core):
    return index // 16 * 64 + low * 32 + index % 16 * 2 + core


def prepare_kernel(*refs, scale, rows):
    *q_refs, lines_ref, starts_ref, most_ref = refs
    mine = lax.axis_index(GROUP)
    depth = lines_ref.shape[0] // 2
    half = lines_ref.shape[1] // len(q_refs)
    most = jnp.float32(0.0)
    for slot, q_ref in enumerate(q_refs):
        source = mine ^ slot
        raw = q_ref[0:depth, :].astype(jnp.float32)
        most = jnp.maximum(most, jnp.max(jnp.sum(raw * raw, axis=0, keepdims=True)))
        scaled = raw * (scale * LOG2E)
        high = scaled.astype(jnp.bfloat16)
        low = (scaled - high.astype(jnp.float32)).astype(jnp.bfloat16)
        at = pl.ds(pl.multiple_of(source * half, half), half)
        lines_ref[0:depth, at] = high
        lines_ref[depth : 2 * depth, at] = low
        digits = q_ref[depth : depth + 16, 0:rows].astype(jnp.float32)
        starts_ref[pl.ds(source, 1), :] = (digits[0:1, :] * 256.0 + digits[1:2, :]).astype(jnp.int32)
    most_ref[...] = jnp.full_like(most_ref, most)


def merge(first, second):
    top = jnp.maximum(first[0:1, :], second[0:1, :])
    total = first[1:2, :] * jnp.exp2(first[0:1, :] - top) + second[1:2, :] * jnp.exp2(second[0:1, :] - top)
    return top, total


def score_kernel(most_ref, starts_ref, lines_ref, keys_ref, *refs, members, heads, rows, scale, swap):
    if swap:
        earlier_ref, sums_ref, stat_ref, merged_ref, mask_ref, part_ref, top_ref = refs
    else:
        sums_ref, stat_ref, mask_ref, part_ref, top_ref = refs
    group = lax.axis_index(PLACE)
    mine = lax.axis_index(GROUP)
    core = lax.axis_index("core")
    side = core ^ swap
    span = CHUNK * BLOCK
    width = heads * rows
    pair = 2 * rows

    largest = jnp.max(jnp.abs(keys_ref[...]), axis=1).astype(jnp.float32)
    longest = jnp.max(jnp.sum(largest * largest, axis=-1))
    safe = jnp.max(most_ref[...]) * longest * (scale * scale) <= SAFE * SAFE
    sums_ref[...] = jnp.zeros_like(sums_ref)

    starts = [starts_ref[2 * member : 2 * member + 1, :] for member in range(members)]
    first_start = jnp.min(functools.reduce(jnp.minimum, starts))
    last_chunk = group // CHUNK
    first_chunk = jnp.minimum(first_start // (rows * 64), last_chunk)

    def chunk_keys(chunk):
        blocks = [keys_ref[column, chunk * 4 + step] for step in range(4) for column in range(4)]
        keys = jnp.concatenate(blocks, axis=0)
        return jnp.concatenate([keys, keys], axis=1)

    line = lax.broadcasted_iota(jnp.int32, (BLOCK, rows), 0)
    places = [
        shard_of(group, member, core) * rows + lax.broadcasted_iota(jnp.int32, (1, rows), 1) for member in range(members)
    ]

    def fill_mask(chunk, causal, inside, outside):
        for block in range(CHUNK):
            base = (shard_of(chunk * CHUNK + block, mine // 2, side) * 2 + mine % 2) * BLOCK
            for member in range(members):
                allowed = line >= starts[member] - base
                if causal:
                    allowed = allowed & (line <= places[member] - base)
                mask_ref[member, block * BLOCK : (block + 1) * BLOCK, :] = jnp.where(allowed, inside, outside)

    def scores(keys, at):
        return jnp.dot(keys, lines_ref[:, pl.ds(at, pair)], preferred_element_type=jnp.float32)

    def lines_of(chunk):
        return pl.ds(pl.multiple_of(chunk * CHUNK, CHUNK), CHUNK)

    @pl.when(safe)
    def _():
        def one_chunk(chunk, carry, causal=False):
            keys = chunk_keys(chunk)
            fill_mask(chunk, causal, 1.0, 0.0)
            for tile in range(members * width // pair):
                at = tile * pair
                result = scores(keys, at)
                for block in range(CHUNK):
                    lines = slice(block * BLOCK, (block + 1) * BLOCK)
                    mask = mask_ref[at // width, lines, :]
                    for column in range(2):
                        x = result[lines, column * rows : (column + 1) * rows]
                        weights = jnp.exp2(x) * mask
                        part_ref[2 * tile + column, block * 8 : block * 8 + 8, :] = jnp.sum(
                            weights.reshape(BLOCK // 8, 8, rows), axis=0
                        )
                for column in range(2):
                    total = part_ref[2 * tile + column, pl.ds(0, CHUNK, stride=8), :]
                    for line in range(1, 8):
                        total = total + part_ref[2 * tile + column, pl.ds(line, CHUNK, stride=8), :]
                    sums_ref[lines_of(chunk), at + column * rows : at + (column + 1) * rows] = total
            return carry

        lax.fori_loop(first_chunk, last_chunk, one_chunk, 0)
        one_chunk(last_chunk, 0, causal=True)

    def each_tile(visit):
        def one_chunk(chunk, carry):
            fill_mask(chunk, True, 0.0, LOW)

            def one_tile(tile, carry):
                at = pl.multiple_of(tile * pair, pair)
                mask = mask_ref[at // width]
                visit(chunk, pl.ds(at, pair), scores(chunk_keys(chunk), at) + jnp.concatenate([mask, mask], axis=1))
                return carry

            return lax.fori_loop(0, members * width // pair, one_tile, carry)

        lax.fori_loop(first_chunk, last_chunk + 1, one_chunk, 0)

    @pl.when(jnp.logical_not(safe))
    def _():
        def raise_top(chunk, at, x):
            top_ref[:, at] = jnp.maximum(top_ref[:, at], jnp.max(x, axis=0, keepdims=True))

        def add(chunk, at, x):
            weights = jnp.where(x > 0.5 * LOW, jnp.exp2(jnp.minimum(x - top_ref[:, at], 0.0)), 0.0)
            sums_ref[lines_of(chunk), at] = jnp.sum(weights.reshape(CHUNK, BLOCK, pair), axis=1)

        top_ref[...] = jnp.full_like(top_ref, LOW)
        each_tile(raise_top)
        each_tile(add)

    total = jnp.sum(sums_ref[...], axis=0, keepdims=True)
    top = jnp.where(safe, jnp.zeros_like(total), top_ref[...])
    stat_ref[0:1, :] = jnp.where(total > 0.0, top, LOW)
    stat_ref[1:2, :] = total
    if swap:
        merged_ref[0:1, :], merged_ref[1:2, :] = merge(stat_ref[...], earlier_ref[...])


def mass_kernel(own_ref, other_ref, own_stat_ref, other_stat_ref, stat_ref, mass_ref, *, members, heads, rows):
    top = jnp.max(stat_ref[:, 0, :], axis=0, keepdims=True)
    total = jnp.sum(stat_ref[:, 1, :] * jnp.exp2(stat_ref[:, 0, :] - top), axis=0, keepdims=True)
    tops = (own_stat_ref[0:1, :], other_stat_ref[0:1, :])
    for side, sums_ref in enumerate((own_ref, other_ref)):
        share = jnp.exp2(tops[side] - top) / total
        for member in range(members):
            mass = None
            for head in range(heads):
                at = (member * heads + head) * rows
                term = sums_ref[:, at : at + rows] * share[:, at : at + rows]
                mass = term if mass is None else mass + term
            for run in range(mass_ref.shape[1]):
                mass_ref[member, run, side] = mass[run * 16 : run * 16 + 16, :]


def target_kernel(mass_ref, ws_ref, out_ref, lines_ref, *, devices, rows, heads):
    core = lax.axis_index("core")
    first = shard_of(lax.axis_index(PLACE), lax.axis_index("yl"), core) * rows
    place = first + lax.broadcasted_iota(jnp.int32, (1, rows), 1)
    visible = (place // BLOCK - ws_ref[...] // BLOCK + 1).astype(jnp.float32) * (1.0 / heads)
    for source in range(devices):
        for run in range(mass_ref.shape[1]):
            for side in range(2):
                begin = 2 * shard_of(run * 16, source // 2, core ^ side) + source % 2
                lines_ref[pl.ds(begin, 16, stride=4), :] = mass_ref[source, run, side] * visible
    out_ref[...] = lines_ref[...].T


GROUP = ("yl", "head")
PLACE = ("yh", "zh", "x")


def spread(x, axes):
    copies = jnp.broadcast_to(x[None], (lax.axis_size(axes), *x.shape))
    return lax.all_to_all(copies, axes, 0, 0, tiled=True)


def body(queries, keys, window_start):
    blocks = lax.axis_size(PLACE)
    devices = lax.axis_size(GROUP)
    members = devices // 2
    rows, heads_here, width = queries.shape
    heads = 2 * heads_here
    scale = 1.0 / math.sqrt(width)

    lines = jnp.transpose(queries, (2, 1, 0)).reshape(width, heads_here * rows)
    digits = jnp.stack([window_start // 256, window_start % 256]).astype(jnp.bfloat16)
    digits = jnp.pad(digits, ((0, 14), (0, (heads_here - 1) * rows)))
    lines = jnp.concatenate([lines, digits], axis=0)

    def trade(x, step):
        return lax.ppermute(x, GROUP, [(i, i ^ step) for i in range(devices)])

    own = lax.dynamic_slice_in_dim(keys, lax.axis_index("head") * BLOCK, BLOCK, 0)
    column, lines, near = lax.optimization_barrier((spread(own, ("yh", "zh")), lines, trade(lines, 1)))
    own_keys = spread(column, "x")
    across, along = trade(lines, 3), trade(lines, 2)
    all_queries = [lines, near, along, across]

    total_rows = members * heads * rows
    vmem = pl.BlockSpec(memory_space=pltpu.VMEM)
    params = pltpu.CompilerParams(vmem_limit_bytes=32 * 1024 * 1024)

    query_lines, starts, most = pl.pallas_call(
        functools.partial(prepare_kernel, scale=scale, rows=rows),
        out_shape=(
            jax.ShapeDtypeStruct((2 * width, total_rows), jnp.bfloat16),
            jax.ShapeDtypeStruct((devices, rows), jnp.int32),
            jax.ShapeDtypeStruct((8, rows), jnp.float32),
        ),
        in_specs=[vmem] * devices,
        out_specs=(vmem, vmem, vmem),
        compiler_params=params,
        cost_estimate=pl.CostEstimate(flops=10 * width * total_rows, bytes_accessed=2 * 1024 * 1024, transcendentals=0),
        name="prepare",
    )(*all_queries)

    own_keys, query_lines = lax.optimization_barrier((own_keys, query_lines))
    other_keys = lax.ppermute(own_keys, "core", [(0, 1), (1, 0)])

    stat_shape = jax.ShapeDtypeStruct((2, total_rows), jnp.float32)

    def score(half_keys, *earlier):
        return pl.pallas_call(
            functools.partial(
                score_kernel, members=members, heads=heads, rows=rows, scale=scale, swap=len(earlier)
            ),
            out_shape=(jax.ShapeDtypeStruct((blocks, total_rows), jnp.float32), stat_shape) + (stat_shape,) * len(earlier),
            in_specs=[vmem] * (4 + len(earlier)),
            out_specs=(vmem,) * (2 + len(earlier)),
            scratch_shapes=[
                pltpu.VMEM((members, CHUNK * BLOCK, rows), jnp.float32),
                pltpu.VMEM((total_rows // rows, CHUNK * 8, rows), jnp.float32),
                pltpu.VMEM((1, total_rows), jnp.float32),
            ],
            compiler_params=params,
            cost_estimate=pl.CostEstimate(
                flops=2 * blocks * BLOCK * width * total_rows,
                bytes_accessed=8 * 1024 * 1024,
                transcendentals=blocks * BLOCK * total_rows,
            ),
            name="score",
        )(most, starts, query_lines, half_keys, *earlier)

    own_sums, own_stat = score(own_keys)
    other_sums, other_stat, stat = score(other_keys, own_stat)
    stats = spread(stat, GROUP)
    mass = pl.pallas_call(
        functools.partial(mass_kernel, members=members, heads=heads, rows=rows),
        out_shape=jax.ShapeDtypeStruct((members, blocks // 16, 2, 16, rows), jnp.float32),
        in_specs=[vmem] * 5,
        out_specs=vmem,
        compiler_params=params,
        name="mass",
    )(own_sums, other_sums, own_stat, other_stat, stats)
    mass = mass.reshape(devices, blocks // 32, 2, 16, rows)
    mass = lax.all_to_all(mass, GROUP, 0, 0, tiled=True)
    return pl.pallas_call(
        functools.partial(target_kernel, devices=devices, rows=rows, heads=heads),
        out_shape=jax.ShapeDtypeStruct((rows, blocks * devices), jnp.float32),
        in_specs=[vmem] * 2,
        out_specs=vmem,
        scratch_shapes=[pltpu.VMEM((blocks * devices, rows), jnp.float32)],
        compiler_params=params,
        name="target",
    )(mass, window_start.reshape(1, rows))


def solution(mesh):
    grid = Mesh(mesh.devices.reshape(-1, 2, 4, 4, 2, 2), ("yh", "yl", "zh", "x", "core", "head"))
    seq = ("yh", "yl", "zh", "x", "core")
    placed = (P(seq, "head", None), P(seq, None), P(seq))
    return jax.shard_map(body, mesh=grid, in_specs=placed, out_specs=P(seq, "head"), check_vma=False)
```

```python
import functools
import math

import jax
import jax.numpy as jnp
import numpy as np
from jax import lax
from jax.experimental import pallas as pl
from jax.experimental.pallas import tpu as pltpu
from jax.sharding import Mesh, PartitionSpec as P

BLOCK = 64
CHUNK = 16
LOW = -1e30
LOG2E = math.log2(math.e)
SAFE = 60.0


def shard_of(index, low, core):
    return index // 16 * 64 + low * 32 + index % 16 * 2 + core


def prepare_kernel(*refs, scale, rows):
    *q_refs, lines_ref, starts_ref, most_ref = refs
    mine = lax.axis_index(GROUP)
    depth = lines_ref.shape[0] // 2
    half = lines_ref.shape[1] // len(q_refs)
    most = jnp.float32(0.0)
    for slot, q_ref in enumerate(q_refs):
        source = mine ^ slot
        raw = q_ref[0:depth, :].astype(jnp.float32)
        most = jnp.maximum(most, jnp.max(jnp.sum(raw * raw, axis=0, keepdims=True)))
        scaled = raw * (scale * LOG2E)
        high = scaled.astype(jnp.bfloat16)
        low = (scaled - high.astype(jnp.float32)).astype(jnp.bfloat16)
        at = pl.ds(pl.multiple_of(source * half, half), half)
        lines_ref[0:depth, at] = high
        lines_ref[depth : 2 * depth, at] = low
        digits = q_ref[depth : depth + 16, 0:rows].astype(jnp.float32)
        starts_ref[pl.ds(source, 1), :] = (digits[0:1, :] * 256.0 + digits[1:2, :]).astype(jnp.int32)
    most_ref[...] = jnp.full_like(most_ref, most)


def merge(first, second):
    top = jnp.maximum(first[0:1, :], second[0:1, :])
    total = first[1:2, :] * jnp.exp2(first[0:1, :] - top) + second[1:2, :] * jnp.exp2(second[0:1, :] - top)
    return top, total


def score_kernel(most_ref, starts_ref, lines_ref, keys_ref, *refs, members, heads, rows, scale, swap):
    if swap:
        earlier_ref, sums_ref, stat_ref, merged_ref, mask_ref, part_ref, top_ref = refs
    else:
        sums_ref, stat_ref, mask_ref, part_ref, top_ref = refs
    group = lax.axis_index(PLACE)
    mine = lax.axis_index(GROUP)
    core = lax.axis_index("core")
    side = core ^ swap
    span = CHUNK * BLOCK
    width = heads * rows
    pair = 2 * rows

    largest = jnp.max(jnp.abs(keys_ref[...]), axis=1).astype(jnp.float32)
    longest = jnp.max(jnp.sum(largest * largest, axis=-1))
    safe = jnp.max(most_ref[...]) * longest * (scale * scale) <= SAFE * SAFE

    starts = [starts_ref[2 * member : 2 * member + 1, :] for member in range(members)]
    first_start = jnp.min(functools.reduce(jnp.minimum, starts))
    last_chunk = group // CHUNK
    first_chunk = jnp.minimum(first_start // (rows * 64), last_chunk)

    def chunk_keys(chunk):
        blocks = [keys_ref[column, chunk * 4 + step] for step in range(4) for column in range(4)]
        keys = jnp.concatenate(blocks, axis=0)
        return jnp.concatenate([keys, keys], axis=1)

    line = lax.broadcasted_iota(jnp.int32, (BLOCK, rows), 0)
    places = [
        shard_of(group, member, core) * rows + lax.broadcasted_iota(jnp.int32, (1, rows), 1) for member in range(members)
    ]

    def fill_mask(chunk, causal, inside, outside):
        for block in range(CHUNK):
            base = (shard_of(chunk * CHUNK + block, mine // 2, side) * 2 + mine % 2) * BLOCK
            for member in range(members):
                allowed = line >= starts[member] - base
                if causal:
                    allowed = allowed & (line <= places[member] - base)
                mask_ref[member, block * BLOCK : (block + 1) * BLOCK, :] = jnp.where(allowed, inside, outside)

    def scores(keys, at):
        return jnp.dot(keys, lines_ref[:, pl.ds(at, pair)], preferred_element_type=jnp.float32)

    def lines_of(chunk):
        return pl.ds(pl.multiple_of(chunk * CHUNK, CHUNK), CHUNK)

    def clear(chunk, carry):
        sums_ref[lines_of(chunk), :] = jnp.zeros((CHUNK, sums_ref.shape[1]), jnp.float32)
        return carry

    lax.fori_loop(0, first_chunk, clear, 0)
    lax.fori_loop(last_chunk + 1, sums_ref.shape[0] // CHUNK, clear, 0)

    @pl.when(safe)
    def _():
        def one_chunk(chunk, carry, causal=False):
            keys = chunk_keys(chunk)
            fill_mask(chunk, causal, 1.0, 0.0)
            for tile in range(members * width // pair):
                at = tile * pair
                result = scores(keys, at)
                for block in range(CHUNK):
                    lines = slice(block * BLOCK, (block + 1) * BLOCK)
                    mask = mask_ref[at // width, lines, :]
                    for column in range(2):
                        x = result[lines, column * rows : (column + 1) * rows]
                        weights = jnp.exp2(x) * mask
                        part_ref[2 * tile + column, block * 8 : block * 8 + 8, :] = jnp.sum(
                            weights.reshape(BLOCK // 8, 8, rows), axis=0
                        )
                for column in range(2):
                    total = part_ref[2 * tile + column, pl.ds(0, CHUNK, stride=8), :]
                    for line in range(1, 8):
                        total = total + part_ref[2 * tile + column, pl.ds(line, CHUNK, stride=8), :]
                    sums_ref[lines_of(chunk), at + column * rows : at + (column + 1) * rows] = total
            return carry

        lax.fori_loop(first_chunk, last_chunk, one_chunk, 0)
        one_chunk(last_chunk, 0, causal=True)

    def each_tile(visit):
        def one_chunk(chunk, carry):
            fill_mask(chunk, True, 0.0, LOW)

            def one_tile(tile, carry):
                at = pl.multiple_of(tile * pair, pair)
                mask = mask_ref[at // width]
                visit(chunk, pl.ds(at, pair), scores(chunk_keys(chunk), at) + jnp.concatenate([mask, mask], axis=1))
                return carry

            return lax.fori_loop(0, members * width // pair, one_tile, carry)

        lax.fori_loop(first_chunk, last_chunk + 1, one_chunk, 0)

    @pl.when(jnp.logical_not(safe))
    def _():
        def raise_top(chunk, at, x):
            top_ref[:, at] = jnp.maximum(top_ref[:, at], jnp.max(x, axis=0, keepdims=True))

        def add(chunk, at, x):
            weights = jnp.where(x > 0.5 * LOW, jnp.exp2(jnp.minimum(x - top_ref[:, at], 0.0)), 0.0)
            sums_ref[lines_of(chunk), at] = jnp.sum(weights.reshape(CHUNK, BLOCK, pair), axis=1)

        top_ref[...] = jnp.full_like(top_ref, LOW)
        each_tile(raise_top)
        each_tile(add)

    total = jnp.sum(sums_ref[...], axis=0, keepdims=True)
    top = jnp.where(safe, jnp.zeros_like(total), top_ref[...])
    stat_ref[0:1, :] = jnp.where(total > 0.0, top, LOW)
    stat_ref[1:2, :] = total
    if swap:
        merged_ref[0:1, :], merged_ref[1:2, :] = merge(stat_ref[...], earlier_ref[...])


def mass_kernel(own_ref, other_ref, own_stat_ref, other_stat_ref, stat_ref, mass_ref, *, members, heads, rows):
    top = jnp.max(stat_ref[:, 0, :], axis=0, keepdims=True)
    total = jnp.sum(stat_ref[:, 1, :] * jnp.exp2(stat_ref[:, 0, :] - top), axis=0, keepdims=True)
    tops = (own_stat_ref[0:1, :], other_stat_ref[0:1, :])
    for side, sums_ref in enumerate((own_ref, other_ref)):
        share = jnp.exp2(tops[side] - top) / total
        for member in range(members):
            mass = None
            for head in range(heads):
                at = (member * heads + head) * rows
                term = sums_ref[:, at : at + rows] * share[:, at : at + rows]
                mass = term if mass is None else mass + term
            for run in range(mass_ref.shape[1]):
                mass_ref[member, run, side] = mass[run * 16 : run * 16 + 16, :]


def target_kernel(mass_ref, ws_ref, out_ref, lines_ref, *, devices, rows, heads):
    core = lax.axis_index("core")
    first = shard_of(lax.axis_index(PLACE), lax.axis_index("yl"), core) * rows
    place = first + lax.broadcasted_iota(jnp.int32, (1, rows), 1)
    visible = (place // BLOCK - ws_ref[...] // BLOCK + 1).astype(jnp.float32) * (1.0 / heads)
    for source in range(devices):
        for run in range(mass_ref.shape[1]):
            for side in range(2):
                begin = 2 * shard_of(run * 16, source // 2, core ^ side) + source % 2
                lines_ref[pl.ds(begin, 16, stride=4), :] = mass_ref[source, run, side] * visible
    out_ref[...] = lines_ref[...].T


GROUP = ("yl", "head")
PLACE = ("yh", "zh", "x")


def spread(x, axes):
    copies = jnp.broadcast_to(x[None], (lax.axis_size(axes), *x.shape))
    return lax.all_to_all(copies, axes, 0, 0, tiled=True)


def body(queries, keys, window_start):
    blocks = lax.axis_size(PLACE)
    devices = lax.axis_size(GROUP)
    members = devices // 2
    rows, heads_here, width = queries.shape
    heads = 2 * heads_here
    scale = 1.0 / math.sqrt(width)

    lines = jnp.transpose(queries, (2, 1, 0)).reshape(width, heads_here * rows)
    digits = jnp.stack([window_start // 256, window_start % 256]).astype(jnp.bfloat16)
    digits = jnp.pad(digits, ((0, 14), (0, (heads_here - 1) * rows)))
    lines = jnp.concatenate([lines, digits], axis=0)

    def trade(x, step):
        return lax.ppermute(x, GROUP, [(i, i ^ step) for i in range(devices)])

    own = lax.dynamic_slice_in_dim(keys, lax.axis_index("head") * BLOCK, BLOCK, 0)
    column, lines, near = lax.optimization_barrier((spread(own, ("yh", "zh")), lines, trade(lines, 1)))
    own_keys = spread(column, "x")
    across, along = trade(lines, 3), trade(lines, 2)
    all_queries = [lines, near, along, across]

    total_rows = members * heads * rows
    vmem = pl.BlockSpec(memory_space=pltpu.VMEM)
    params = pltpu.CompilerParams(vmem_limit_bytes=32 * 1024 * 1024)

    query_lines, starts, most = pl.pallas_call(
        functools.partial(prepare_kernel, scale=scale, rows=rows),
        out_shape=(
            jax.ShapeDtypeStruct((2 * width, total_rows), jnp.bfloat16),
            jax.ShapeDtypeStruct((devices, rows), jnp.int32),
            jax.ShapeDtypeStruct((8, rows), jnp.float32),
        ),
        in_specs=[vmem] * devices,
        out_specs=(vmem, vmem, vmem),
        compiler_params=params,
        cost_estimate=pl.CostEstimate(flops=10 * width * total_rows, bytes_accessed=2 * 1024 * 1024, transcendentals=0),
        name="prepare",
    )(*all_queries)

    own_keys, query_lines = lax.optimization_barrier((own_keys, query_lines))
    other_keys = lax.ppermute(own_keys, "core", [(0, 1), (1, 0)])

    stat_shape = jax.ShapeDtypeStruct((2, total_rows), jnp.float32)

    def score(half_keys, *earlier):
        return pl.pallas_call(
            functools.partial(
                score_kernel, members=members, heads=heads, rows=rows, scale=scale, swap=len(earlier)
            ),
            out_shape=(jax.ShapeDtypeStruct((blocks, total_rows), jnp.float32), stat_shape) + (stat_shape,) * len(earlier),
            in_specs=[vmem] * (4 + len(earlier)),
            out_specs=(vmem,) * (2 + len(earlier)),
            scratch_shapes=[
                pltpu.VMEM((members, CHUNK * BLOCK, rows), jnp.float32),
                pltpu.VMEM((total_rows // rows, CHUNK * 8, rows), jnp.float32),
                pltpu.VMEM((1, total_rows), jnp.float32),
            ],
            compiler_params=params,
            cost_estimate=pl.CostEstimate(
                flops=2 * blocks * BLOCK * width * total_rows,
                bytes_accessed=8 * 1024 * 1024,
                transcendentals=blocks * BLOCK * total_rows,
            ),
            name="score",
        )(most, starts, query_lines, half_keys, *earlier)

    own_sums, own_stat = score(own_keys)
    other_sums, other_stat, stat = score(other_keys, own_stat)
    stats = spread(stat, GROUP)
    mass = pl.pallas_call(
        functools.partial(mass_kernel, members=members, heads=heads, rows=rows),
        out_shape=jax.ShapeDtypeStruct((members, blocks // 16, 2, 16, rows), jnp.float32),
        in_specs=[vmem] * 5,
        out_specs=vmem,
        compiler_params=params,
        name="mass",
    )(own_sums, other_sums, own_stat, other_stat, stats)
    mass = mass.reshape(devices, blocks // 32, 2, 16, rows)
    mass = lax.all_to_all(mass, GROUP, 0, 0, tiled=True)
    return pl.pallas_call(
        functools.partial(target_kernel, devices=devices, rows=rows, heads=heads),
        out_shape=jax.ShapeDtypeStruct((rows, blocks * devices), jnp.float32),
        in_specs=[vmem] * 2,
        out_specs=vmem,
        scratch_shapes=[pltpu.VMEM((blocks * devices, rows), jnp.float32)],
        compiler_params=params,
        name="target",
    )(mass, window_start.reshape(1, rows))


def solution(mesh):
    grid = Mesh(mesh.devices.reshape(-1, 2, 4, 4, 2, 2), ("yh", "yl", "zh", "x", "core", "head"))
    seq = ("yh", "yl", "zh", "x", "core")
    placed = (P(seq, "head", None), P(seq, None), P(seq))
    return jax.shard_map(body, mesh=grid, in_specs=placed, out_specs=P(seq, "head"), check_vma=False)
```
